512 devices in a mesh: dp: 64 (over x, y_lo, z), tensor: 8 (over y_hi, core).
Axes of the slice: x: 4, y: 8 (y_hi: 4, y_lo: 2; y = y_hi * 2 + y_lo), z: 8, core: 2. Of those that a mesh axis runs over, the one named last changes fastest.
Arguments:
- acts: bfloat16 [8192, 4096], P('dp', 'tensor'), may hold values from -410 to 410
- grads_out: bfloat16 [8192, 32768], P('dp', 'tensor'), may hold values from -410 to 410
- grad: bfloat16 [4096, 32768], P('tensor', 'dp'), may hold values from -6 to 6
Outputs:
- precond: float32 [4096, 32768], P('tensor', 'dp')
The draws below stay inside these ranges and needn't reach their ends.
All inputs are finite; a program needn't handle non-finite values.
Results may differ from the reference program's by a relative error of at most 0.0012.
The reference program's roundings to bfloat16 on the way count: a program that leaves them out, or rounds other values in their place, can miss the bound.
Values may be sent and summed in bfloat16 or wider, within the bound.
No kernel may reach another device: no remote copies, remote signals or barrier semaphores. Data moves between devices by JAX's collectives and lax.ppermute only.
A program may use at most 64 MiB of HBM per device.

```python
import math
import jax
import jax.numpy as jnp
from jax import lax

BLOCK = 512
NEWTON = 2
D = 4096
FF = 32768
TOKENS = 8192


latent_pool = 256


terms_each = 8


def feature_draw(key, row_count, col_count, scale_low, scale_high):
    key_noise, key_scale, key_latent, key_chosen, key_flip, key_loading = jax.random.split(key, 6)
    base_noise = 0.7 * jax.random.truncated_normal(key_noise, -4.0, 4.0, (row_count, col_count), jnp.float32)
    col_scale = jnp.exp(jax.random.uniform(key_scale, (1, col_count), jnp.float32, math.log(scale_low), math.log(scale_high)))
    latent = jax.random.truncated_normal(key_latent, -3.0, 3.0, (row_count, latent_pool), jnp.float32)
    amplitude = jnp.power(jnp.arange(latent_pool, dtype=jnp.float32) + 1.0, -0.25)
    weighted = latent * amplitude[None, :]
    chosen_latent = jax.random.randint(key_chosen, (terms_each, col_count), 0, latent_pool)
    sign_flip = (jax.random.randint(key_flip, (terms_each, col_count), 0, 2) * 2 - 1).astype(jnp.float32)
    loadings = sign_flip * jax.random.uniform(key_loading, (terms_each, col_count), jnp.float32, 0.75, 1.5)
    values = base_noise
    for term_index in range(terms_each):
        values = values + jnp.take(weighted, chosen_latent[term_index], axis=1) * loadings[term_index][None, :]
    return col_scale * values


def draw_acts(key, part):
    key = jax.random.fold_in(key, 11)
    values = feature_draw(key, TOKENS, D, 0.3, 3.0)
    return values.astype(jnp.bfloat16)


def draw_grads_out(key, part):
    key = jax.random.fold_in(key, 23)
    values = feature_draw(key, TOKENS, FF, 0.3, 3.0)
    return values.astype(jnp.bfloat16)


def levels(stream_key, extent, pieces, low, high):
    gain, own = 1.0, jax.random.fold_in(stream_key, 6)
    for position, parts in pieces:
        steps = jnp.exp(jax.random.uniform(jax.random.fold_in(own, position), (parts,), jnp.float32, low / len(pieces), high / len(pieces)))
        gain = gain * jnp.repeat(steps, extent[position] // parts).reshape([-1 if axis == position else 1 for axis in range(len(extent))])
    return gain


def gaussian(stream_key, shape, width, limit, cuts=(), kind=jnp.bfloat16):
    entries = width * jax.random.normal(stream_key, shape, jnp.float32)
    if cuts:
        entries = entries * levels(stream_key, shape, cuts, -0.22, 0.18)
    return jnp.clip(entries, -limit, limit).astype(kind)


def setup_inputs(seed: int = 0) -> dict:
    key_list = jax.random.split(jax.random.key(seed), 4)
    acts = draw_acts(jax.random.fold_in(key_list[3], 71), 0)
    grads_out = draw_grads_out(jax.random.fold_in(key_list[3], 71), 0)
    grad = gaussian(key_list[2], (D, FF), 1.0, 6.0, ((0, 8), (1, 64)))
    return {"acts": acts, "grads_out": grads_out, "grad": grad}


DAMPING = 0.1
PRECISE = lax.Precision.HIGHEST

def inverse_root(covariance):
    width_all = covariance.shape[0]
    identity = jnp.eye(width_all, dtype=jnp.float32)
    shifted = covariance / TOKENS + DAMPING * identity
    frob_norm = jnp.sqrt(jnp.sum(shifted * shifted))
    iterate_y = shifted / frob_norm
    iterate_z = identity
    for iteration in range(NEWTON):
        update = 1.5 * identity - 0.5 * jnp.dot(iterate_z, iterate_y, precision=PRECISE, preferred_element_type=jnp.float32)
        if iteration + 1 < NEWTON:
            iterate_y = jnp.dot(update, iterate_y, precision=PRECISE, preferred_element_type=jnp.float32)
        iterate_z = jnp.dot(update, iterate_z, precision=PRECISE, preferred_element_type=jnp.float32)
    return (iterate_z / jnp.sqrt(frob_norm)).astype(jnp.bfloat16)

def block_roots(data):
    count_blocks = data.shape[1] // BLOCK
    blocks = jnp.transpose(data.reshape(TOKENS, count_blocks, BLOCK), (1, 0, 2))

    def one_block(piece):
        return inverse_root(jnp.dot(piece.T, piece, preferred_element_type=jnp.float32))
    return lax.map(one_block, blocks)

def reference(acts, grads_out, grad):
    act_roots = block_roots(acts)
    grad_roots = block_roots(grads_out)
    count_a = D // BLOCK
    count_g = FF // BLOCK
    tiles = grad.reshape(count_a, BLOCK, count_g, BLOCK).astype(jnp.float32)
    left_side = jnp.einsum('iab,ibjc->iajc', act_roots.astype(jnp.float32), tiles, precision=PRECISE).astype(jnp.bfloat16)
    result = jnp.einsum('iajc,jcd->iajd', left_side.astype(jnp.float32), grad_roots.astype(jnp.float32), precision=PRECISE)
    return result.reshape(D, FF)
```

```python
import jax
import jax.numpy as jnp
import numpy as np
from jax import lax
from jax.experimental import pallas as pl
from jax.experimental.pallas import tpu as pltpu
from jax.sharding import Mesh, PartitionSpec as P

TOKENS = 8192
DAMPING = 0.1
BLOCK = 512
TILE = 128
SIDE = BLOCK // TILE
TILES = [(a, b) for a in range(SIDE) for b in range(a, SIDE)]
PACKED = len(TILES) * TILE
PEERS = 8
SHARE = PACKED // PEERS
PIECE = 24
RAW = SIDE * TILE
FIRST = RAW + 2 * SHARE
SECOND = SHARE + PIECE
BF16, F32 = jnp.bfloat16, jnp.float32
AXES = ("x", "yl", "z", "yh", "c")
SIZES = (4, 2, 8, 4, 2)
VMEM = pl.BlockSpec(memory_space=pltpu.VMEM)
PARAMS = pltpu.CompilerParams(vmem_limit_bytes=24 * 1024 * 1024)


def gram(data):
    return lax.dot_general(data, data, (((0,), (0,)), ((), ())), preferred_element_type=F32)


def store_packed(total, store):
    for place, (a, b) in enumerate(TILES):
        store(place * TILE, total[a * TILE : (a + 1) * TILE, b * TILE : (b + 1) * TILE])


def unpack(packed, full):
    for place, (a, b) in enumerate(TILES):
        tile = packed(place * TILE)
        full[a * TILE : (a + 1) * TILE, b * TILE : (b + 1) * TILE] = tile
        if a != b:
            full[b * TILE : (b + 1) * TILE, a * TILE : (a + 1) * TILE] = tile.T


def halves(values):
    high = values.astype(BF16)
    return high, (values - high.astype(F32)).astype(BF16)


def product(left, right):
    left_high, left_low = left
    right_high, right_low = right
    dot = lambda p, q: jnp.dot(p, q, preferred_element_type=F32)
    return dot(left_high, right_high) + (dot(left_high, right_low) + dot(left_low, right_high))


def inverse_root(covariance):
    rows = lax.broadcasted_iota(jnp.int32, (BLOCK, BLOCK), 0)
    columns = lax.broadcasted_iota(jnp.int32, (BLOCK, BLOCK), 1)
    diagonal = rows == columns
    shifted = covariance * (1.0 / TOKENS) + jnp.where(diagonal, DAMPING, 0.0)
    squares = jnp.sum(jnp.sum(shifted * shifted, axis=0, keepdims=True), axis=1, keepdims=True)
    frob = jnp.sqrt(squares)
    y = shifted * (1.0 / frob)
    y_halves = halves(y)
    s = product(y_halves, y_halves)
    tail = product(halves(s), halves(0.0625 * s - 0.5625 * y))
    z = jnp.where(diagonal, 2.25, 0.0) - 2.4375 * y + 1.6875 * s + tail
    return (z * (1.0 / jnp.sqrt(frob))).astype(BF16)


def first_kernel(acts, grads, out, packed):
    def keep(row, tile):
        packed[row : row + TILE, :] = tile

    store_packed(gram(acts[...]), keep)
    for peer in range(PEERS):
        for part in range(SIDE):
            column = peer * BLOCK + part * TILE
            out[peer, part * TILE : (part + 1) * TILE, :] = grads[:, column : column + TILE]
        high, low = halves(packed[peer * SHARE : (peer + 1) * SHARE, :])
        out[peer, RAW : RAW + SHARE, :] = high
        out[peer, RAW + SHARE : FIRST, :] = low


def second_kernel(got, out, packed, share):
    tokens = jnp.concatenate(
        [got[:, p * TILE : (p + 1) * TILE, :].reshape(PEERS * TILE, TILE) for p in range(SIDE)],
        axis=1,
    )

    def keep(row, tile):
        packed[row : row + TILE, :] = tile

    store_packed(gram(tokens), keep)
    total = jnp.zeros((SHARE, TILE), F32)
    for peer in range(PEERS):
        high = got[peer, RAW : RAW + SHARE, :].astype(F32)
        total += high + got[peer, RAW + SHARE : FIRST, :].astype(F32)
    share[0:SHARE, :] = total
    share[SHARE:, :] = jnp.zeros((PEERS * PIECE - SHARE, TILE), F32)
    for peer in range(PEERS):
        out[peer, 0:SHARE, :] = packed[peer * SHARE : (peer + 1) * SHARE, :]
        out[peer, SHARE:SECOND, :] = share[peer * PIECE : (peer + 1) * PIECE, :]


def sum_kernel(got, out):
    total = got[0]
    for peer in range(1, PEERS):
        total += got[peer]
    for peer in range(PEERS):
        out[peer] = total


def root_kernel(got, root, out, packed, share, full):
    for peer in range(PEERS):
        packed[peer * SHARE : (peer + 1) * SHARE, :] = got[peer, 0:SHARE, :]
        share[peer * PIECE : (peer + 1) * PIECE, :] = got[peer, SHARE:SECOND, :]
    unpack(lambda row: packed[row : row + TILE, :], full)
    root[...] = inverse_root(full[...])
    for peer in range(PEERS):
        out[peer] = share[0:SHARE, :]


def last_kernel(got, grad, grad_root, out, full):
    unpack(lambda row: got[row : row + TILE, :], full)
    act_root = inverse_root(full[...])
    left = jnp.dot(act_root, grad[...], preferred_element_type=F32).astype(BF16)
    out[...] = jnp.dot(left, grad_root[...], preferred_element_type=F32)


def call(kernel, count, outs, scratch, flops):
    return pl.pallas_call(
        kernel,
        out_shape=outs,
        in_specs=[VMEM] * count,
        out_specs=[VMEM] * len(outs),
        scratch_shapes=scratch,
        compiler_params=PARAMS,
        cost_estimate=pl.CostEstimate(flops=flops, bytes_accessed=4 << 20, transcendentals=0),
    )


def shape(dims, dtype):
    return jax.ShapeDtypeStruct(dims, dtype)


def exchange(data, axes):
    return lax.all_to_all(data, axes, split_axis=0, concat_axis=0, tiled=True)


def transposition():
    places = np.arange(np.prod(SIZES)).reshape(SIZES)
    return [
        (int(places[x, yl, z, yh, c]), int(places[yh, c, z, x, yl]))
        for x, yl, z, yh, c in np.ndindex(*SIZES)
    ]


def on_device(acts, grads_out, grad):
    cube = 2 * BLOCK**3
    packed = pltpu.VMEM((PACKED, TILE), F32)
    share = pltpu.VMEM((PEERS * PIECE, TILE), F32)
    full = pltpu.VMEM((BLOCK, BLOCK), F32)
    (sent,) = call(first_kernel, 2, [shape((PEERS, FIRST, TILE), BF16)], [packed], cube // 4)(
        acts, grads_out
    )
    got = exchange(sent, "z")
    (sent,) = call(second_kernel, 1, [shape((PEERS, SECOND, TILE), F32)], [packed, share], 2 * cube)(
        got
    )
    got = exchange(sent, ("x", "yl"))
    (sent,) = call(sum_kernel, 1, [shape((PEERS, SECOND, TILE), F32)], [], 1 << 20)(got)
    got = exchange(sent, ("x", "yl"))
    root, sent = call(
        root_kernel,
        1,
        [shape((BLOCK, BLOCK), BF16), shape((PEERS, SHARE, TILE), F32)],
        [packed, share, full],
        6 * cube,
    )(got)
    grad_root = lax.ppermute(root, AXES, transposition())
    got = exchange(sent, "z")
    (out,) = call(last_kernel, 3, [shape((BLOCK, BLOCK), F32)], [full], 8 * cube)(
        got.reshape(PACKED, TILE), grad, grad_root
    )
    return out


def solution(mesh):
    split = Mesh(mesh.devices.reshape(SIZES), AXES)
    dp, tensor = AXES[:3], AXES[3:]
    return jax.shard_map(
        on_device,
        mesh=split,
        in_specs=(P(dp, tensor), P(dp, tensor), P(tensor, dp)),
        out_specs=P(tensor, dp),
        check_vma=False,
    )
```

```python
import functools

import jax
import jax.numpy as jnp
import numpy as np
from jax import lax
from jax.experimental import pallas as pl
from jax.experimental.pallas import tpu as pltpu
from jax.sharding import Mesh, PartitionSpec as P

TOKENS = 8192
DAMPING = 0.1
BLOCK = 512
TILE = 128
SIDE = BLOCK // TILE
TILES = [(a, b) for a in range(SIDE) for b in range(a, SIDE)]
PACKED = len(TILES) * TILE
HALF = PACKED // 2
PEERS = 8
SHARE = PACKED // PEERS
BF16, F32 = jnp.bfloat16, jnp.float32
AXES = ("x", "yl", "z", "yh", "c")
SIZES = (4, 2, 8, 4, 2)
VMEM = pl.BlockSpec(memory_space=pltpu.VMEM)
ANYWHERE = pl.BlockSpec(memory_space=pl.ANY)
PARAMS = pltpu.CompilerParams(vmem_limit_bytes=24 * 1024 * 1024)


def gram(data):
    return lax.dot_general(data, data, (((0,), (0,)), ((), ())), preferred_element_type=F32)


def pack(total, packed):
    for place, (a, b) in enumerate(TILES):
        tile = total[a * TILE : (a + 1) * TILE, b * TILE : (b + 1) * TILE]
        packed[place * TILE : (place + 1) * TILE, :] = tile


def unpack(packed, full):
    for place, (a, b) in enumerate(TILES):
        tile = packed[place * TILE : (place + 1) * TILE, :]
        full[a * TILE : (a + 1) * TILE, b * TILE : (b + 1) * TILE] = tile
        if a != b:
            full[b * TILE : (b + 1) * TILE, a * TILE : (a + 1) * TILE] = tile.T


def rows(bit, count):
    return pl.ds(pl.multiple_of(bit * count, count), count)


def halves(values):
    high = values.astype(BF16)
    return high, (values - high.astype(F32)).astype(BF16)


def product(left, right):
    left_high, left_low = left
    right_high, right_low = right
    dot = lambda p, q: jnp.dot(p, q, preferred_element_type=F32)
    return dot(left_high, right_high) + (dot(left_high, right_low) + dot(left_low, right_high))


def inverse_root(covariance):
    row = lax.broadcasted_iota(jnp.int32, (BLOCK, BLOCK), 0)
    column = lax.broadcasted_iota(jnp.int32, (BLOCK, BLOCK), 1)
    diagonal = row == column
    shifted = covariance * (1.0 / TOKENS) + jnp.where(diagonal, DAMPING, 0.0)
    squares = jnp.sum(jnp.sum(shifted * shifted, axis=0, keepdims=True), axis=1, keepdims=True)
    frob = jnp.sqrt(squares)
    y = shifted * (1.0 / frob)
    y_halves = halves(y)
    s = product(y_halves, y_halves)
    tail = product(halves(s), halves(0.0625 * s - 0.5625 * y))
    z = jnp.where(diagonal, 2.25, 0.0) - 2.4375 * y + 1.6875 * s + tail
    return (z * (1.0 / jnp.sqrt(frob))).astype(BF16)


def split_kernel(grads, out):
    for peer in range(PEERS):
        out[peer] = grads[:, peer * BLOCK : (peer + 1) * BLOCK]


def act_gram_kernel(acts, keep, send, packed):
    pack(gram(acts[...]), packed)
    bit = lax.axis_index("yl")
    keep[...] = packed[rows(bit, HALF), :]
    send[...] = packed[rows(1 - bit, HALF), :]


def halve_kernel(digit, kept, got, keep, send):
    bit = lax.rem(lax.axis_index("x") // digit, 2)
    count = keep.shape[0]
    keep[...] = kept[rows(bit, count), :] + got[rows(bit, count), :]
    send[...] = kept[rows(1 - bit, count), :] + got[rows(1 - bit, count), :]


def add_kernel(kept, got, out):
    out[...] = kept[...] + got[...]


def copies_kernel(kept, got, out):
    total = kept[...] + got[...]
    for peer in range(PEERS):
        out[peer] = total


def grad_gram_kernel(got, out):
    pack(gram(got[...].reshape(PEERS * TILE, BLOCK)), out)


def sum_kernel(got, out):
    total = got[0]
    for peer in range(1, PEERS):
        total += got[peer]
    for peer in range(PEERS):
        out[peer] = total


def grad_root_kernel(got, out, full, packed):
    unpack(got, full)
    pack(inverse_root(full[...]), packed)
    out[...] = packed[rows(lax.axis_index("yl"), HALF), :]


def left_kernel(got, grad, out, packed, full):
    for x, yl in np.ndindex(4, 2):
        start = (yl * 4 + x) * SHARE
        packed[start : start + SHARE, :] = got[x * 2 + yl]
    unpack(packed, full)
    root = inverse_root(full[...])
    out[...] = jnp.dot(root, grad[...], preferred_element_type=F32).astype(BF16)


def last_kernel(left, mine, other, out, packed, full):
    bit = lax.axis_index("c")
    packed[rows(bit, HALF), :] = mine[...]
    packed[rows(1 - bit, HALF), :] = other[...]
    unpack(packed, full)
    out[...] = jnp.dot(left[...], full[...], preferred_element_type=F32)


def call(kernel, args, outs, scratch=(), flops=1 << 20, after=()):
    outs = [jax.ShapeDtypeStruct(dims, dtype) for dims, dtype in outs]
    data = sum(a.size * a.dtype.itemsize for a in [*args, *outs])

    def body(*refs):
        kernel(*refs[: len(args)], *refs[len(args) + len(after) :])

    got = pl.pallas_call(
        body,
        out_shape=outs,
        in_specs=[VMEM] * len(args) + [ANYWHERE] * len(after),
        out_specs=[VMEM] * len(outs),
        scratch_shapes=[pltpu.VMEM(dims, dtype) for dims, dtype in scratch],
        compiler_params=PARAMS,
        cost_estimate=pl.CostEstimate(flops=flops, bytes_accessed=data, transcendentals=0),
    )(*args, *after)
    return got if len(outs) > 1 else got[0]


def exchange(data, axes):
    return lax.all_to_all(data, axes, split_axis=0, concat_axis=0, tiled=True)


def swap(data, axis, size, distance):
    return lax.ppermute(data, axis, [(i, i ^ distance) for i in range(size)])


def transpose_places(data):
    places = np.arange(np.prod(SIZES)).reshape(SIZES)
    pairs = [
        (int(places[x, yl, z, yh, c]), int(places[yh, c, z, (x + yh) % 4, yl]))
        for x, yl, z, yh, c in np.ndindex(*SIZES)
    ]
    return lax.ppermute(data, AXES, pairs)


def on_device(acts, grads_out, grad):
    cube = 2 * BLOCK**3
    packed, full = (PACKED, TILE), (BLOCK, BLOCK)
    copies = (PEERS, SHARE, TILE)

    split = call(split_kernel, [grads_out], [((PEERS, TILE, BLOCK), BF16)])
    tokens = exchange(split, "z")

    half = [((HALF, TILE), F32)] * 2
    keep, send = call(act_gram_kernel, [acts], half, [(packed, F32)], cube // 4, [split])
    got = swap(send, "yl", 2, 1)
    quarter = [((HALF // 2, TILE), F32)] * 2
    keep, send = call(functools.partial(halve_kernel, 2), [keep, got], quarter)
    got = swap(send, "x", 4, 2)
    eighth = [((SHARE, TILE), F32)] * 2
    keep, send = call(functools.partial(halve_kernel, 1), [keep, got], eighth)
    got = swap(send, "x", 4, 1)
    share_xy = call(add_kernel, [keep, got], eighth[:1])
    part = call(grad_gram_kernel, [tokens], [(packed, F32)], (), 2 * cube, [share_xy])

    got = swap(share_xy, "z", 8, 1)
    share = call(add_kernel, [share_xy, got], eighth[:1], after=[part])
    got = swap(share, "z", 8, 2)
    share_z = call(add_kernel, [share, got], eighth[:1])
    parts = exchange(part.reshape(copies), ("x", "yl"))
    sent = call(sum_kernel, [parts], [(copies, F32)], after=[share_z])

    got = swap(share_z, "z", 8, 4)
    act_sent = call(copies_kernel, [share_z, got], [(copies, F32)], after=[sent])
    grad_cov = exchange(sent, ("x", "yl")).reshape(packed)
    root = call(
        grad_root_kernel,
        [grad_cov],
        [((HALF, TILE), BF16)],
        [(full, F32), (packed, BF16)],
        6 * cube,
        [act_sent],
    )
    mine = transpose_places(root)

    act_cov = exchange(act_sent, ("x", "yl"))
    left = call(
        left_kernel, [act_cov, grad], [(full, BF16)], [(packed, F32), (full, F32)], 7 * cube
    )
    other = swap(mine, "c", 2, 1)
    return call(
        last_kernel, [left, mine, other], [(full, F32)], [(packed, BF16), (full, BF16)], cube
    )


def solution(mesh):
    split = Mesh(mesh.devices.reshape(SIZES), AXES)
    dp, tensor = AXES[:3], AXES[3:]
    return jax.shard_map(
        on_device,
        mesh=split,
        in_specs=(P(dp, tensor), P(dp, tensor), P(tensor, dp)),
        out_specs=P(tensor, dp),
        check_vma=False,
    )
```

```python
import jax
import jax.numpy as jnp
import numpy as np
from jax import lax
from jax.experimental import pallas as pl
from jax.experimental.pallas import tpu as pltpu
from jax.sharding import Mesh, PartitionSpec as P

TOKENS = 8192
DAMPING = 0.1
BLOCK = 512
TILE = 128
SIDE = BLOCK // TILE
TILES = [(a, b) for a in range(SIDE) for b in range(a, SIDE)]
PACKED = len(TILES) * TILE
HALF = PACKED // 2
PEERS = 8
SHARE = PACKED // PEERS
BF16, F32 = jnp.bfloat16, jnp.float32
AXES = ("x", "yl", "z", "yh", "c")
SIZES = (4, 2, 8, 4, 2)
VMEM = pl.BlockSpec(memory_space=pltpu.VMEM)
ANYWHERE = pl.BlockSpec(memory_space=pl.ANY)
PARAMS = pltpu.CompilerParams(vmem_limit_bytes=24 * 1024 * 1024)


def gram(data):
    return lax.dot_general(data, data, (((0,), (0,)), ((), ())), preferred_element_type=F32)


def pack(total, packed):
    for place, (a, b) in enumerate(TILES):
        tile = total[a * TILE : (a + 1) * TILE, b * TILE : (b + 1) * TILE]
        packed[place * TILE : (place + 1) * TILE, :] = tile


def unpack(packed, full):
    for place, (a, b) in enumerate(TILES):
        tile = packed[place * TILE : (place + 1) * TILE, :]
        full[a * TILE : (a + 1) * TILE, b * TILE : (b + 1) * TILE] = tile
        if a != b:
            full[b * TILE : (b + 1) * TILE, a * TILE : (a + 1) * TILE] = tile.T


def rows(bit, count):
    return pl.ds(pl.multiple_of(bit * count, count), count)


def halves(values):
    high = values.astype(BF16)
    return high, (values - high.astype(F32)).astype(BF16)


def product(left, right):
    left_high, left_low = left
    right_high, right_low = right
    dot = lambda p, q: jnp.dot(p, q, preferred_element_type=F32)
    return dot(left_high, right_high) + (dot(left_high, right_low) + dot(left_low, right_high))


def inverse_root(covariance):
    row = lax.broadcasted_iota(jnp.int32, (BLOCK, BLOCK), 0)
    column = lax.broadcasted_iota(jnp.int32, (BLOCK, BLOCK), 1)
    diagonal = row == column
    shifted = covariance * (1.0 / TOKENS) + jnp.where(diagonal, DAMPING, 0.0)
    squares = jnp.sum(jnp.sum(shifted * shifted, axis=0, keepdims=True), axis=1, keepdims=True)
    frob = jnp.sqrt(squares)
    y = shifted * (1.0 / frob)
    y_halves = halves(y)
    s = product(y_halves, y_halves)
    tail = product(halves(s), halves(0.0625 * s - 0.5625 * y))
    z = jnp.where(diagonal, 2.25, 0.0) - 2.4375 * y + 1.6875 * s + tail
    return (z * (1.0 / jnp.sqrt(frob))).astype(BF16)


def split_kernel(grads, out, sems):
    moves = [
        pltpu.make_async_copy(
            grads.at[:, pl.ds(peer * BLOCK, BLOCK)], out.at[peer], sems.at[peer]
        )
        for peer in range(PEERS)
    ]
    for move in moves:
        move.start()
    for move in moves:
        move.wait()


def act_gram_kernel(mine, other, keep, send, packed):
    pack(gram(jnp.concatenate([mine[...], other[...]], axis=0)), packed)
    count = keep.shape[0]
    start = 2 * lax.axis_index("yl")
    bit = lax.axis_index("x") // 2
    keep[...] = packed[rows(start + bit, count), :]
    send[...] = packed[rows(start + 1 - bit, count), :]


def halve_kernel(kept, got, keep, send):
    bit = lax.rem(lax.axis_index("x"), 2)
    count = keep.shape[0]
    keep[...] = kept[rows(bit, count), :] + got[rows(bit, count), :]
    send[...] = kept[rows(1 - bit, count), :] + got[rows(1 - bit, count), :]


def add_kernel(kept, got, out):
    out[...] = kept[...] + got[...]


def add_four_kernel(kept, second, third, fourth, out):
    out[...] = (kept[...] + second[...]) + (third[...] + fourth[...])


def grad_gram_kernel(got, out):
    pack(gram(got[...].reshape(PEERS * TILE, BLOCK)), out)


def sum_kernel(got, share, out, copies):
    total = got[0]
    for peer in range(1, PEERS):
        total += got[peer]
    out[...] = total
    for peer in range(PEERS):
        copies[peer] = share[...]


def join_kernel(*refs):
    *parts, out = refs
    for place, part in enumerate(parts):
        out[place] = part[...]


def left_kernel(got, grad, out, packed, full):
    for x, yl in np.ndindex(4, 2):
        start = (yl * 4 + x) * SHARE
        packed[start : start + SHARE, :] = got[x * 2 + yl]
    unpack(packed, full)
    root = inverse_root(full[...])
    out[...] = jnp.dot(root, grad[...], preferred_element_type=F32).astype(BF16)


def last_kernel(left, mine, other, out, packed, full):
    bit = lax.axis_index("c")
    turn = lax.axis_index("yh") - lax.axis_index("x") + 4
    for step in range(4):
        owner = 2 * lax.rem(turn + 4 - step, 4)
        packed[rows(owner + bit, SHARE), :] = mine[step]
        packed[rows(owner + 1 - bit, SHARE), :] = other[step]
    unpack(packed, full)
    root = inverse_root(full[...])
    out[...] = jnp.dot(left[...], root, preferred_element_type=F32)


def call(kernel, args, outs, scratch=(), flops=1 << 20, after=()):
    outs = [jax.ShapeDtypeStruct(dims, dtype) for dims, dtype in outs]
    data = sum(a.size * a.dtype.itemsize for a in [*args, *outs])

    def body(*refs):
        kernel(*refs[: len(args)], *refs[len(args) + len(after) :])

    got = pl.pallas_call(
        body,
        out_shape=outs,
        in_specs=[VMEM] * len(args) + [ANYWHERE] * len(after),
        out_specs=[VMEM] * len(outs),
        scratch_shapes=[pltpu.VMEM(dims, dtype) for dims, dtype in scratch],
        compiler_params=PARAMS,
        cost_estimate=pl.CostEstimate(flops=flops, bytes_accessed=data, transcendentals=0),
    )(*args, *after)
    return got if len(outs) > 1 else got[0]


def exchange(data, axes):
    return lax.all_to_all(data, axes, split_axis=0, concat_axis=0, tiled=True)


def swap(data, axis, size, distance):
    return lax.ppermute(data, axis, [(i, i ^ distance) for i in range(size)])


def to_column(data, step):
    places = np.arange(np.prod(SIZES)).reshape(SIZES)
    pairs = [
        (int(places[x, yl, z, yh, c]), int(places[yh, c, z, (x + yh + step) % 4, yl]))
        for x, yl, z, yh, c in np.ndindex(*SIZES)
    ]
    return lax.ppermute(data, AXES, pairs)


def on_device(acts, grads_out, grad):
    cube = 2 * BLOCK**3
    packed, full = (PACKED, TILE), (BLOCK, BLOCK)
    copies = (PEERS, SHARE, TILE)

    split = pl.pallas_call(
        split_kernel,
        out_shape=jax.ShapeDtypeStruct((PEERS, TILE, BLOCK), BF16),
        in_specs=[ANYWHERE],
        out_specs=ANYWHERE,
        scratch_shapes=[pltpu.SemaphoreType.DMA((PEERS,))],
        cost_estimate=pl.CostEstimate(flops=0, bytes_accessed=2 << 20, transcendentals=0),
    )(grads_out)
    tokens = exchange(split, "z")

    other = swap(acts, "yl", 2, 1)
    quarter = [((HALF // 2, TILE), F32)] * 2
    keep, send = call(act_gram_kernel, [acts, other], quarter, [(packed, F32)], cube // 2)
    got = swap(send, "x", 4, 2)
    eighth = [((SHARE, TILE), F32)] * 2
    keep, send = call(halve_kernel, [keep, got], eighth)
    got = swap(send, "x", 4, 1)
    share = call(add_kernel, [keep, got], eighth[:1])
    got = swap(share, "z", 8, 1)
    share = call(add_kernel, [share, got], eighth[:1])
    part = call(grad_gram_kernel, [tokens], [(packed, F32)], (), 2 * cube, [share])

    got = [swap(share, "z", 8, distance) for distance in (2, 4, 6)]
    share = call(add_four_kernel, [share, *got], eighth[:1], after=[part])
    parts = exchange(part.reshape(copies), ("x", "yl"))
    grad_share, act_sent = call(
        sum_kernel, [parts, share], [((SHARE, TILE), F32), (copies, F32)]
    )
    joined = [((4, SHARE, TILE), F32)]
    mine = call(join_kernel, [to_column(grad_share, step) for step in range(4)], joined)
    other = swap(mine, "c", 2, 1)

    act_cov = exchange(act_sent, ("x", "yl"))
    left = call(
        left_kernel, [act_cov, grad], [(full, BF16)], [(packed, F32), (full, F32)], 7 * cube
    )
    return call(
        last_kernel, [left, mine, other], [(full, F32)], [(packed, F32), (full, F32)], 7 * cube
    )


def solution(mesh):
    split = Mesh(mesh.devices.reshape(SIZES), AXES)
    dp, tensor = AXES[:3], AXES[3:]
    return jax.shard_map(
        on_device,
        mesh=split,
        in_specs=(P(dp, tensor), P(dp, tensor), P(tensor, dp)),
        out_specs=P(tensor, dp),
        check_vma=False,
    )
```

```python
import jax
import jax.numpy as jnp
import numpy as np
from jax import lax
from jax.experimental import pallas as pl
from jax.experimental.pallas import tpu as pltpu
from jax.sharding import Mesh, PartitionSpec as P

TOKENS = 8192
DAMPING = 0.1
BLOCK = 512
TILE = 128
SIDE = BLOCK // TILE
TILES = [(a, b) for a in range(SIDE) for b in range(a, SIDE)]
PACKED = len(TILES) * TILE
HALF = PACKED // 2
PEERS = 8
SHARE = PACKED // PEERS
PIECE = 24
RAW = SIDE * TILE
DIAGONAL = 8
FIRST = RAW + SHARE + 2 * DIAGONAL
GATHER = SHARE + PIECE
SECOND = GATHER + DIAGONAL
BF16, F32 = jnp.bfloat16, jnp.float32
AXES = ("x", "yl", "z", "yh", "c")
SIZES = (4, 2, 8, 4, 2)
VMEM = pl.BlockSpec(memory_space=pltpu.VMEM)
PARAMS = pltpu.CompilerParams(vmem_limit_bytes=24 * 1024 * 1024)


def gram(data):
    return lax.dot_general(data, data, (((0,), (0,)), ((), ())), preferred_element_type=F32)


def pack(total, packed):
    for place, (a, b) in enumerate(TILES):
        tile = total[a * TILE : (a + 1) * TILE, b * TILE : (b + 1) * TILE]
        packed[place * TILE : (place + 1) * TILE, :] = tile


def unpack(packed, full):
    for place, (a, b) in enumerate(TILES):
        tile = packed[place * TILE : (place + 1) * TILE, :].astype(full.dtype)
        full[a * TILE : (a + 1) * TILE, b * TILE : (b + 1) * TILE] = tile
        if a != b:
            full[b * TILE : (b + 1) * TILE, a * TILE : (a + 1) * TILE] = tile.T


def rows(bit, count):
    return pl.ds(pl.multiple_of(bit * count, count), count)


def halves(values):
    high = values.astype(BF16)
    return high, (values - high.astype(F32)).astype(BF16)


def product(left, right):
    left_high, left_low = left
    right_high, right_low = right
    dot = lambda p, q: jnp.dot(p, q, preferred_element_type=F32)
    return dot(left_high, right_high) + (dot(left_high, right_low) + dot(left_low, right_high))


def on_diagonal(count):
    row = lax.broadcasted_iota(jnp.int32, (count, count), 0)
    return row == lax.broadcasted_iota(jnp.int32, (count, count), 1)


def diagonals(total):
    parts = []
    for a in range(SIDE):
        tile = total[a * TILE : (a + 1) * TILE, a * TILE : (a + 1) * TILE]
        parts.append(jnp.sum(jnp.where(on_diagonal(TILE), tile, 0.0), axis=0, keepdims=True))
    return jnp.concatenate(parts + [jnp.zeros((DIAGONAL - SIDE, TILE), F32)], axis=0)


def inverse_root(covariance):
    diagonal = on_diagonal(BLOCK)
    shifted = covariance * (1.0 / TOKENS) + jnp.where(diagonal, DAMPING, 0.0)
    squares = jnp.sum(jnp.sum(shifted * shifted, axis=0, keepdims=True), axis=1, keepdims=True)
    frob = jnp.sqrt(squares)
    y = shifted * (1.0 / frob)
    y_halves = halves(y)
    s = product(y_halves, y_halves)
    tail = product(halves(s), halves(0.0625 * s - 0.5625 * y))
    z = jnp.where(diagonal, 2.25, 0.0) - 2.4375 * y + 1.6875 * s + tail
    return (z * (1.0 / jnp.sqrt(frob))).astype(BF16)


def first_kernel(acts, grads, out, packed):
    total = gram(acts[...])
    pack(total, packed)
    high, low = halves(diagonals(total))
    ends = jnp.concatenate([high, low], axis=0)
    for peer in range(PEERS):
        for part in range(SIDE):
            column = peer * BLOCK + part * TILE
            out[peer, part * TILE : (part + 1) * TILE, :] = grads[:, column : column + TILE]
        share = packed[peer * SHARE : (peer + 1) * SHARE, :]
        out[peer, RAW : RAW + SHARE, :] = share.astype(BF16)
        out[peer, RAW + SHARE : FIRST, :] = ends


def second_kernel(got, out, packed, share):
    tokens = jnp.concatenate(
        [got[:, p * TILE : (p + 1) * TILE, :].reshape(PEERS * TILE, TILE) for p in range(SIDE)],
        axis=1,
    )
    pack(gram(tokens), packed)
    total = jnp.zeros((SHARE, TILE), F32)
    ends = jnp.zeros((2 * DIAGONAL, TILE), F32)
    for peer in range(PEERS):
        total += got[peer, RAW : RAW + SHARE, :].astype(F32)
        ends += got[peer, RAW + SHARE : FIRST, :].astype(F32)
    share[0:SHARE, :] = total
    share[SHARE:, :] = jnp.zeros((PEERS * PIECE - SHARE, TILE), F32)
    for peer in range(PEERS):
        out[peer, 0:SHARE, :] = packed[peer * SHARE : (peer + 1) * SHARE, :]
        out[peer, SHARE:GATHER, :] = share[peer * PIECE : (peer + 1) * PIECE, :]
        out[peer, GATHER:SECOND, :] = ends[0:DIAGONAL] + ends[DIAGONAL:]


def sum_kernel(got, out, ends):
    total = got[0]
    for peer in range(1, PEERS):
        total += got[peer]
    for peer in range(PEERS):
        out[peer] = total[0:GATHER]
    ends[...] = total[GATHER:SECOND]


def grad_root_kernel(got, out, copies, full, packed, half, share):
    for peer in range(PEERS):
        packed[peer * SHARE : (peer + 1) * SHARE, :] = got[peer, 0:SHARE, :]
        share[peer * PIECE : (peer + 1) * PIECE, :] = got[peer, SHARE:GATHER, :]
    unpack(packed, full)
    pack(inverse_root(full[...]), half)
    out[...] = half[rows(lax.axis_index("yl"), HALF), :]
    for peer in range(PEERS):
        copies[peer] = share[0:SHARE, :].astype(BF16)


def left_kernel(got, ends, grad, out, full):
    unpack(got, full)
    for a in range(SIDE):
        place = slice(a * TILE, (a + 1) * TILE)
        full[place, place] = jnp.where(on_diagonal(TILE), ends[a : a + 1, :], full[place, place])
    root = inverse_root(full[...])
    out[...] = jnp.dot(root, grad[...], preferred_element_type=F32).astype(BF16)


def last_kernel(left, mine, other, out, packed, full):
    bit = lax.axis_index("c")
    packed[rows(bit, HALF), :] = mine[...]
    packed[rows(1 - bit, HALF), :] = other[...]
    unpack(packed, full)
    out[...] = jnp.dot(left[...], full[...], preferred_element_type=F32)


def call(kernel, args, outs, scratch=(), flops=1 << 20):
    outs = [jax.ShapeDtypeStruct(dims, dtype) for dims, dtype in outs]
    data = sum(a.size * a.dtype.itemsize for a in [*args, *outs])
    got = pl.pallas_call(
        kernel,
        out_shape=outs,
        in_specs=[VMEM] * len(args),
        out_specs=[VMEM] * len(outs),
        scratch_shapes=[pltpu.VMEM(dims, dtype) for dims, dtype in scratch],
        compiler_params=PARAMS,
        cost_estimate=pl.CostEstimate(flops=flops, bytes_accessed=data, transcendentals=0),
    )(*args)
    return got if len(outs) > 1 else got[0]


def exchange(data, axes):
    return lax.all_to_all(data, axes, split_axis=0, concat_axis=0, tiled=True)


def swap(data, axis, size, distance):
    return lax.ppermute(data, axis, [(i, i ^ distance) for i in range(size)])


def transpose_places(data):
    places = np.arange(np.prod(SIZES)).reshape(SIZES)
    pairs = [
        (int(places[x, yl, z, yh, c]), int(places[yh, c, z, (x + yh) % 4, yl]))
        for x, yl, z, yh, c in np.ndindex(*SIZES)
    ]
    return lax.ppermute(data, AXES, pairs)


def on_device(acts, grads_out, grad):
    cube = 2 * BLOCK**3
    packed, full = (PACKED, TILE), (BLOCK, BLOCK)

    share = (PEERS * PIECE, TILE)
    sent = call(
        first_kernel,
        [acts, grads_out],
        [((PEERS, FIRST, TILE), BF16)],
        [(packed, F32)],
        cube // 4,
    )
    got = exchange(sent, "z")
    sent = call(
        second_kernel,
        [got],
        [((PEERS, SECOND, TILE), F32)],
        [(packed, F32), (share, F32)],
        2 * cube,
    )
    got = exchange(sent, ("x", "yl"))
    sent, ends = call(
        sum_kernel, [got], [((PEERS, GATHER, TILE), F32), ((DIAGONAL, TILE), F32)]
    )
    got = exchange(sent, ("x", "yl"))
    root, sent = call(
        grad_root_kernel,
        [got],
        [((HALF, TILE), BF16), ((PEERS, SHARE, TILE), BF16)],
        [(full, F32), (packed, F32), (packed, BF16), (share, F32)],
        6 * cube,
    )
    mine = transpose_places(root)
    act_cov = exchange(sent, "z").reshape(packed)
    left = call(left_kernel, [act_cov, ends, grad], [(full, BF16)], [(full, F32)], 7 * cube)
    other = swap(mine, "c", 2, 1)
    return call(
        last_kernel, [left, mine, other], [(full, F32)], [(packed, BF16), (full, BF16)], cube
    )


def solution(mesh):
    split = Mesh(mesh.devices.reshape(SIZES), AXES)
    dp, tensor = AXES[:3], AXES[3:]
    return jax.shard_map(
        on_device,
        mesh=split,
        in_specs=(P(dp, tensor), P(dp, tensor), P(tensor, dp)),
        out_specs=P(tensor, dp),
        check_vma=False,
    )
```

```python
import jax
import jax.numpy as jnp
import numpy as np
from jax import lax
from jax.experimental import pallas as pl
from jax.experimental.pallas import tpu as pltpu
from jax.sharding import Mesh, PartitionSpec as P

TOKENS = 8192
DAMPING = 0.1
BLOCK = 512
TILE = 128
SIDE = BLOCK // TILE
TILES = [(a, b) for a in range(SIDE) for b in range(a, SIDE)]
PACKED = len(TILES) * TILE
HALF = PACKED // 2
PEERS = 8
SHARE = PACKED // PEERS
PIECE = 32
RAW = SIDE * TILE
DIAGONAL = 8
FIRST = RAW + SHARE + 2 * DIAGONAL
GATHER = SHARE + PIECE
SECOND = GATHER + PIECE + 4 * DIAGONAL
BF16, F32 = jnp.bfloat16, jnp.float32
AXES = ("x", "yl", "z", "yh", "c")
SIZES = (4, 2, 8, 4, 2)
VMEM = pl.BlockSpec(memory_space=pltpu.VMEM)
ANYWHERE = pl.BlockSpec(memory_space=pl.ANY)
PARAMS = pltpu.CompilerParams(vmem_limit_bytes=24 * 1024 * 1024)


def gram(data):
    return lax.dot_general(data, data, (((0,), (0,)), ((), ())), preferred_element_type=F32)


def pack(total, packed):
    for place, (a, b) in enumerate(TILES):
        tile = total[a * TILE : (a + 1) * TILE, b * TILE : (b + 1) * TILE]
        packed[place * TILE : (place + 1) * TILE, :] = tile


def unpack(packed, full):
    for place, (a, b) in enumerate(TILES):
        tile = packed[place * TILE : (place + 1) * TILE, :].astype(full.dtype)
        full[a * TILE : (a + 1) * TILE, b * TILE : (b + 1) * TILE] = tile
        if a != b:
            full[b * TILE : (b + 1) * TILE, a * TILE : (a + 1) * TILE] = tile.T


def rows(bit, count):
    return pl.ds(pl.multiple_of(bit * count, count), count)


def halves(values):
    high = values.astype(BF16)
    return high, (values - high.astype(F32)).astype(BF16)


def product(left, right):
    left_high, left_low = left
    right_high, right_low = right
    dot = lambda p, q: jnp.dot(p, q, preferred_element_type=F32)
    return dot(left_high, right_high) + (dot(left_high, right_low) + dot(left_low, right_high))


def on_diagonal(count):
    row = lax.broadcasted_iota(jnp.int32, (count, count), 0)
    return row == lax.broadcasted_iota(jnp.int32, (count, count), 1)


def diagonals(total):
    parts = []
    for a in range(SIDE):
        tile = total[a * TILE : (a + 1) * TILE, a * TILE : (a + 1) * TILE]
        parts.append(jnp.sum(jnp.where(on_diagonal(TILE), tile, 0.0), axis=0, keepdims=True))
    return jnp.concatenate(parts + [jnp.zeros((DIAGONAL - SIDE, TILE), F32)], axis=0)


def inverse_root(covariance):
    diagonal = on_diagonal(BLOCK)
    shifted = covariance * (1.0 / TOKENS) + jnp.where(diagonal, DAMPING, 0.0)
    squares = jnp.sum(jnp.sum(shifted * shifted, axis=0, keepdims=True), axis=1, keepdims=True)
    frob = jnp.sqrt(squares)
    y = shifted * (1.0 / frob)
    y_halves = halves(y)
    s = product(y_halves, y_halves)
    tail = product(halves(s), halves(0.0625 * s - 0.5625 * y))
    z = jnp.where(diagonal, 2.25, 0.0) - 2.4375 * y + 1.6875 * s + tail
    return (z * (1.0 / jnp.sqrt(frob))).astype(BF16)


def first_kernel(acts, grads, out, packed):
    total = gram(acts[...])
    pack(total, packed)
    high, low = halves(diagonals(total))
    ends = jnp.concatenate([high, low], axis=0)
    for peer in range(PEERS):
        for part in range(SIDE):
            column = peer * BLOCK + part * TILE
            out[peer, part * TILE : (part + 1) * TILE, :] = grads[:, column : column + TILE]
        share = packed[peer * SHARE : (peer + 1) * SHARE, :]
        out[peer, RAW : RAW + SHARE, :] = share.astype(BF16)
        out[peer, RAW + SHARE : FIRST, :] = ends


def second_kernel(got, out, packed, share):
    tokens = jnp.concatenate(
        [got[:, p * TILE : (p + 1) * TILE, :].reshape(PEERS * TILE, TILE) for p in range(SIDE)],
        axis=1,
    )
    grad_total = gram(tokens)
    pack(grad_total, packed)
    total = jnp.zeros((SHARE, TILE), F32)
    ends = jnp.zeros((2 * DIAGONAL, TILE), F32)
    for peer in range(PEERS):
        total += got[peer, RAW : RAW + SHARE, :].astype(F32)
        ends += got[peer, RAW + SHARE : FIRST, :].astype(F32)
    share[0:SHARE, :] = total
    share[SHARE:, :] = jnp.zeros((PEERS * PIECE - SHARE, TILE), F32)
    grad_ends = halves(diagonals(grad_total))
    act_ends = halves(ends[0:DIAGONAL] + ends[DIAGONAL:])
    both = jnp.concatenate([*grad_ends, *act_ends], axis=0)
    for peer in range(PEERS):
        high, low = halves(share[peer * PIECE : (peer + 1) * PIECE, :])
        out[peer, 0:SHARE, :] = packed[peer * SHARE : (peer + 1) * SHARE, :].astype(BF16)
        out[peer, SHARE:GATHER, :] = high
        out[peer, GATHER : GATHER + PIECE, :] = low
        out[peer, GATHER + PIECE : SECOND, :] = both


def sum_kernel(got, out, ends):
    total = got[0].astype(F32)
    for peer in range(1, PEERS):
        total += got[peer].astype(F32)
    share = total[0:SHARE].astype(BF16)
    piece = (total[SHARE:GATHER] + total[GATHER : GATHER + PIECE]).astype(BF16)
    for peer in range(PEERS):
        out[peer, 0:SHARE, :] = share
        out[peer, SHARE:GATHER, :] = piece
    both = total[GATHER + PIECE : SECOND]
    ends[0:DIAGONAL, :] = both[0:DIAGONAL] + both[DIAGONAL : 2 * DIAGONAL]
    ends[DIAGONAL:, :] = both[2 * DIAGONAL : 3 * DIAGONAL] + both[3 * DIAGONAL :]


def set_diagonal(full, ends, first):
    for a in range(SIDE):
        place = slice(a * TILE, (a + 1) * TILE)
        exact = ends[first + a : first + a + 1, :]
        full[place, place] = jnp.where(on_diagonal(TILE), exact, full[place, place])


def grad_root_kernel(got, ends, out, full, packed):
    for peer in range(PEERS):
        packed[peer * SHARE : (peer + 1) * SHARE, :] = got[peer, 0:SHARE, :]
    unpack(packed, full)
    set_diagonal(full, ends, 0)
    pack(inverse_root(full[...]), packed)
    out[...] = packed[rows(lax.axis_index("yl"), HALF), :]


def copies_kernel(got, out):
    for place in range(SHARE // PIECE):
        piece = got[place, SHARE:GATHER, :]
        for peer in range(PEERS):
            out[peer, place * PIECE : (place + 1) * PIECE, :] = piece


def left_kernel(got, ends, grad, out, full):
    unpack(got, full)
    set_diagonal(full, ends, DIAGONAL)
    root = inverse_root(full[...])
    out[...] = jnp.dot(root, grad[...], preferred_element_type=F32).astype(BF16)


def last_kernel(left, mine, other, out, packed, full):
    bit = lax.axis_index("c")
    packed[rows(bit, HALF), :] = mine[...]
    packed[rows(1 - bit, HALF), :] = other[...]
    unpack(packed, full)
    out[...] = jnp.dot(left[...], full[...], preferred_element_type=F32)


def call(kernel, args, outs, scratch=(), flops=1 << 20, after=()):
    outs = [jax.ShapeDtypeStruct(dims, dtype) for dims, dtype in outs]
    data = sum(a.size * a.dtype.itemsize for a in [*args, *outs])

    def body(*refs):
        kernel(*refs[: len(args)], *refs[len(args) + len(after) :])

    got = pl.pallas_call(
        body,
        out_shape=outs,
        in_specs=[VMEM] * len(args) + [ANYWHERE] * len(after),
        out_specs=[VMEM] * len(outs),
        scratch_shapes=[pltpu.VMEM(dims, dtype) for dims, dtype in scratch],
        compiler_params=PARAMS,
        cost_estimate=pl.CostEstimate(flops=flops, bytes_accessed=data, transcendentals=0),
    )(*args, *after)
    return got if len(outs) > 1 else got[0]


def exchange(data, axes):
    return lax.all_to_all(data, axes, split_axis=0, concat_axis=0, tiled=True)


def swap(data, axis, size, distance):
    return lax.ppermute(data, axis, [(i, i ^ distance) for i in range(size)])


def transpose_places(data):
    places = np.arange(np.prod(SIZES)).reshape(SIZES)
    pairs = [
        (int(places[x, yl, z, yh, c]), int(places[yh, c, z, (x + yh) % 4, yl]))
        for x, yl, z, yh, c in np.ndindex(*SIZES)
    ]
    return lax.ppermute(data, AXES, pairs)


def on_device(acts, grads_out, grad):
    cube = 2 * BLOCK**3
    packed, full = (PACKED, TILE), (BLOCK, BLOCK)

    share = (PEERS * PIECE, TILE)
    sent = call(
        first_kernel,
        [acts, grads_out],
        [((PEERS, FIRST, TILE), BF16)],
        [(packed, F32)],
        cube // 4,
    )
    got = exchange(sent, "z")
    sent = call(
        second_kernel,
        [got],
        [((PEERS, SECOND, TILE), BF16)],
        [(packed, F32), (share, F32)],
        2 * cube,
    )
    got = exchange(sent, ("x", "yl"))
    sent, ends = call(
        sum_kernel, [got], [((PEERS, GATHER, TILE), BF16), ((2 * DIAGONAL, TILE), F32)]
    )
    got = exchange(sent, ("x", "yl"))
    root = call(
        grad_root_kernel,
        [got, ends],
        [((HALF, TILE), BF16)],
        [(full, F32), (packed, BF16)],
        6 * cube,
    )
    mine = transpose_places(root)
    sent = call(copies_kernel, [got], [((PEERS, SHARE, TILE), BF16)], after=[root])
    act_cov = exchange(sent, "z").reshape(packed)
    left = call(left_kernel, [act_cov, ends, grad], [(full, BF16)], [(full, F32)], 7 * cube)
    other = swap(mine, "c", 2, 1)
    return call(
        last_kernel, [left, mine, other], [(full, F32)], [(packed, BF16), (full, BF16)], cube
    )


def solution(mesh):
    split = Mesh(mesh.devices.reshape(SIZES), AXES)
    dp, tensor = AXES[:3], AXES[3:]
    return jax.shard_map(
        on_device,
        mesh=split,
        in_specs=(P(dp, tensor), P(dp, tensor), P(tensor, dp)),
        out_specs=P(tensor, dp),
        check_vma=False,
    )
```

```python
import jax
import jax.numpy as jnp
import numpy as np
from jax import lax
from jax.experimental import pallas as pl
from jax.experimental.pallas import tpu as pltpu
from jax.sharding import Mesh, PartitionSpec as P

TOKENS = 8192
DAMPING = 0.1
BLOCK = 512
TILE = 128
SIDE = BLOCK // TILE
TILES = [(a, b) for a in range(SIDE) for b in range(a, SIDE)]
PACKED = len(TILES) * TILE
HALF = PACKED // 2
PEERS = 8
SHARE = PACKED // PEERS
RAW = SIDE * TILE
DIAGONAL = 8
FIRST = RAW + SHARE + 2 * DIAGONAL
SECOND = 2 * SHARE + 4 * DIAGONAL
COLUMN = SHARE + 2 * DIAGONAL
BF16, F32 = jnp.bfloat16, jnp.float32
AXES = ("x", "yl", "z", "yh", "c")
SIZES = (4, 2, 8, 4, 2)
VMEM = pl.BlockSpec(memory_space=pltpu.VMEM)
PARAMS = pltpu.CompilerParams(vmem_limit_bytes=24 * 1024 * 1024)


def gram(data):
    return lax.dot_general(data, data, (((0,), (0,)), ((), ())), preferred_element_type=F32)


def pack(total, packed):
    for place, (a, b) in enumerate(TILES):
        tile = total[a * TILE : (a + 1) * TILE, b * TILE : (b + 1) * TILE]
        packed[place * TILE : (place + 1) * TILE, :] = tile


def unpack(packed, full):
    for place, (a, b) in enumerate(TILES):
        tile = packed[place * TILE : (place + 1) * TILE, :].astype(full.dtype)
        full[a * TILE : (a + 1) * TILE, b * TILE : (b + 1) * TILE] = tile
        if a != b:
            full[b * TILE : (b + 1) * TILE, a * TILE : (a + 1) * TILE] = tile.T


def rows(bit, count):
    return pl.ds(pl.multiple_of(bit * count, count), count)


def halves(values):
    high = values.astype(BF16)
    return high, (values - high.astype(F32)).astype(BF16)


def product(left, right):
    left_high, left_low = left
    right_high, right_low = right
    dot = lambda p, q: jnp.dot(p, q, preferred_element_type=F32)
    return dot(left_high, right_high) + (dot(left_high, right_low) + dot(left_low, right_high))


def on_diagonal(count):
    row = lax.broadcasted_iota(jnp.int32, (count, count), 0)
    return row == lax.broadcasted_iota(jnp.int32, (count, count), 1)


def diagonals(total):
    parts = []
    for a in range(SIDE):
        tile = total[a * TILE : (a + 1) * TILE, a * TILE : (a + 1) * TILE]
        parts.append(jnp.sum(jnp.where(on_diagonal(TILE), tile, 0.0), axis=0, keepdims=True))
    return jnp.concatenate(parts + [jnp.zeros((DIAGONAL - SIDE, TILE), F32)], axis=0)


def inverse_root(covariance):
    diagonal = on_diagonal(BLOCK)
    shifted = covariance * (1.0 / TOKENS) + jnp.where(diagonal, DAMPING, 0.0)
    squares = jnp.sum(jnp.sum(shifted * shifted, axis=0, keepdims=True), axis=1, keepdims=True)
    frob = jnp.sqrt(squares)
    y = shifted * (1.0 / frob)
    y_halves = halves(y)
    s = product(y_halves, y_halves)
    tail = product(halves(s), halves(0.0625 * s - 0.5625 * y))
    z = jnp.where(diagonal, 2.25, 0.0) - 2.4375 * y + 1.6875 * s + tail
    return (z * (1.0 / jnp.sqrt(frob))).astype(BF16)


def first_kernel(acts, grads, out, packed):
    total = gram(acts[...])
    pack(total, packed)
    high, low = halves(diagonals(total))
    ends = jnp.concatenate([high, low], axis=0)
    for peer in range(PEERS):
        for part in range(SIDE):
            column = peer * BLOCK + part * TILE
            out[peer, part * TILE : (part + 1) * TILE, :] = grads[:, column : column + TILE]
        share = packed[peer * SHARE : (peer + 1) * SHARE, :]
        out[peer, RAW : RAW + SHARE, :] = share.astype(BF16)
        out[peer, RAW + SHARE : FIRST, :] = ends


def second_kernel(got, out, packed):
    tokens = jnp.concatenate(
        [got[:, p * TILE : (p + 1) * TILE, :].reshape(PEERS * TILE, TILE) for p in range(SIDE)],
        axis=1,
    )
    grad_total = gram(tokens)
    pack(grad_total, packed)
    total = jnp.zeros((SHARE, TILE), F32)
    ends = jnp.zeros((2 * DIAGONAL, TILE), F32)
    for peer in range(PEERS):
        total += got[peer, RAW : RAW + SHARE, :].astype(F32)
        ends += got[peer, RAW + SHARE : FIRST, :].astype(F32)
    act_share = total.astype(BF16)
    grad_ends = halves(diagonals(grad_total))
    act_ends = halves(ends[0:DIAGONAL] + ends[DIAGONAL:])
    both = jnp.concatenate([*grad_ends, *act_ends], axis=0)
    for peer in range(PEERS):
        out[peer, 0:SHARE, :] = packed[peer * SHARE : (peer + 1) * SHARE, :].astype(BF16)
        out[peer, SHARE : 2 * SHARE, :] = act_share
        out[peer, 2 * SHARE : SECOND, :] = both


def sum_kernel(got, grad_share, copies, ends):
    total = got[0].astype(F32)
    for peer in range(1, PEERS):
        total += got[peer].astype(F32)
    act_share = total[SHARE : 2 * SHARE].astype(BF16)
    for peer in range(PEERS):
        copies[peer] = act_share
    both = total[2 * SHARE : SECOND]
    high, low = halves(both[0:DIAGONAL] + both[DIAGONAL : 2 * DIAGONAL])
    grad_share[0:SHARE, :] = total[0:SHARE].astype(BF16)
    grad_share[SHARE:, :] = jnp.concatenate([high, low], axis=0)
    ends[...] = both[2 * DIAGONAL : 3 * DIAGONAL] + both[3 * DIAGONAL :]


def set_diagonal(full, ends):
    for a in range(SIDE):
        place = slice(a * TILE, (a + 1) * TILE)
        full[place, place] = jnp.where(on_diagonal(TILE), ends[a : a + 1, :], full[place, place])


def join_kernel(*refs):
    *parts, out = refs
    for place, part in enumerate(parts):
        out[place] = part[...]


def left_kernel(got, ends, grad, out, full):
    unpack(got, full)
    set_diagonal(full, ends[...])
    root = inverse_root(full[...])
    out[...] = jnp.dot(root, grad[...], preferred_element_type=F32).astype(BF16)


def last_kernel(left, mine, other, out, packed, full):
    bit = lax.axis_index("c")
    turn = lax.axis_index("yh") - lax.axis_index("x") + 4
    for step in range(4):
        owner = 2 * lax.rem(turn + 4 - step, 4)
        packed[rows(owner + bit, SHARE), :] = mine[step, 0:SHARE, :]
        packed[rows(owner + 1 - bit, SHARE), :] = other[step, 0:SHARE, :]
    unpack(packed, full)
    ends = mine[0, SHARE:COLUMN, :].astype(F32)
    set_diagonal(full, ends[0:DIAGONAL] + ends[DIAGONAL:])
    root = inverse_root(full[...])
    out[...] = jnp.dot(left[...], root, preferred_element_type=F32)


def call(kernel, args, outs, scratch=(), flops=1 << 20):
    outs = [jax.ShapeDtypeStruct(dims, dtype) for dims, dtype in outs]
    data = sum(a.size * a.dtype.itemsize for a in [*args, *outs])
    got = pl.pallas_call(
        kernel,
        out_shape=outs,
        in_specs=[VMEM] * len(args),
        out_specs=[VMEM] * len(outs),
        scratch_shapes=[pltpu.VMEM(dims, dtype) for dims, dtype in scratch],
        compiler_params=PARAMS,
        cost_estimate=pl.CostEstimate(flops=flops, bytes_accessed=data, transcendentals=0),
    )(*args)
    return got if len(outs) > 1 else got[0]


def exchange(data, axes):
    return lax.all_to_all(data, axes, split_axis=0, concat_axis=0, tiled=True)


def swap(data, axis, size, distance):
    return lax.ppermute(data, axis, [(i, i ^ distance) for i in range(size)])


def to_column(data, step):
    places = np.arange(np.prod(SIZES)).reshape(SIZES)
    pairs = [
        (int(places[x, yl, z, yh, c]), int(places[yh, c, z, (x + yh + step) % 4, yl]))
        for x, yl, z, yh, c in np.ndindex(*SIZES)
    ]
    return lax.ppermute(data, AXES, pairs)


def on_device(acts, grads_out, grad):
    cube = 2 * BLOCK**3
    packed, full = (PACKED, TILE), (BLOCK, BLOCK)

    sent = call(
        first_kernel,
        [acts, grads_out],
        [((PEERS, FIRST, TILE), BF16)],
        [(packed, F32)],
        cube // 4,
    )
    got = exchange(sent, "z")
    sent = call(
        second_kernel,
        [got],
        [((PEERS, SECOND, TILE), BF16)],
        [(packed, F32)],
        2 * cube,
    )
    got = exchange(sent, ("x", "yl"))
    grad_share, sent, ends = call(
        sum_kernel,
        [got],
        [((COLUMN, TILE), BF16), ((PEERS, SHARE, TILE), BF16), ((DIAGONAL, TILE), F32)],
    )
    parts = [to_column(grad_share, step) for step in range(4)]
    mine = call(join_kernel, parts, [((4, COLUMN, TILE), BF16)])
    other = swap(mine, "c", 2, 1)
    act_cov = exchange(sent, "z").reshape(packed)
    left = call(left_kernel, [act_cov, ends, grad], [(full, BF16)], [(full, F32)], 7 * cube)
    return call(
        last_kernel, [left, mine, other], [(full, F32)], [(packed, BF16), (full, F32)], 7 * cube
    )


def solution(mesh):
    split = Mesh(mesh.devices.reshape(SIZES), AXES)
    dp, tensor = AXES[:3], AXES[3:]
    return jax.shard_map(
        on_device,
        mesh=split,
        in_specs=(P(dp, tensor), P(dp, tensor), P(tensor, dp)),
        out_specs=P(tensor, dp),
        check_vma=False,
    )
```

```python
import jax
import jax.numpy as jnp
import numpy as np
from jax import lax
from jax.experimental import pallas as pl
from jax.experimental.pallas import tpu as pltpu
from jax.sharding import Mesh, PartitionSpec as P

TOKENS = 8192
DAMPING = 0.1
BLOCK = 512
TILE = 128
SIDE = BLOCK // TILE
UPPER = [(a, b) for a in range(SIDE) for b in range(a + 1, SIDE)]
PAIRS = range(0, SIDE, 2)
PACKED = (len(UPPER) + len(PAIRS)) * TILE
HALF = PACKED // 2
PEERS = 8
SHARE = PACKED // PEERS
PIECE = SHARE // PEERS
RAW = SIDE * TILE
DIAGONAL = 8
FIRST = RAW + SHARE + 2 * DIAGONAL
GATHER = SHARE + PIECE
SECOND = GATHER + PIECE + 4 * DIAGONAL
ROOT = HALF + 2 * DIAGONAL
BF16, F32 = jnp.bfloat16, jnp.float32
AXES = ("x", "yl", "z", "yh", "c")
SIZES = (4, 2, 8, 4, 2)
VMEM = pl.BlockSpec(memory_space=pltpu.VMEM)
ANYWHERE = pl.BlockSpec(memory_space=pl.ANY)
PARAMS = pltpu.CompilerParams(vmem_limit_bytes=24 * 1024 * 1024)


def gram(data):
    return lax.dot_general(data, data, (((0,), (0,)), ((), ())), preferred_element_type=F32)


def tile_at(a, b):
    return slice(a * TILE, (a + 1) * TILE), slice(b * TILE, (b + 1) * TILE)


def over_diagonal():
    row = lax.broadcasted_iota(jnp.int32, (TILE, TILE), 0)
    return row < lax.broadcasted_iota(jnp.int32, (TILE, TILE), 1)


def pack(total, packed):
    tiles = [total[tile_at(a, b)] for a, b in UPPER]
    for a in PAIRS:
        first, second = total[tile_at(a, a)], total[tile_at(a + 1, a + 1)]
        tiles.append(jnp.where(over_diagonal(), first, second))
    for place, tile in enumerate(tiles):
        packed[place * TILE : (place + 1) * TILE, :] = tile.astype(packed.dtype)


def unpack(packed, full, ends):
    tiles = [packed[start : start + TILE, :].astype(F32) for start in range(0, PACKED, TILE)]
    for (a, b), tile in zip(UPPER, tiles):
        full[tile_at(a, b)] = tile.astype(full.dtype)
        full[tile_at(b, a)] = tile.T.astype(full.dtype)
    for a, tile in zip(PAIRS, tiles[len(UPPER) :]):
        turned = tile.T
        both = (tile, turned), (turned, tile)
        for place, (above, below) in enumerate(both, start=a):
            whole = jnp.where(over_diagonal(), above, below)
            whole = jnp.where(on_diagonal(TILE), ends[place : place + 1, :], whole)
            full[tile_at(place, place)] = whole.astype(full.dtype)


def rows(bit, count):
    return pl.ds(pl.multiple_of(bit * count, count), count)


def halves(values):
    high = values.astype(BF16)
    return high, (values - high.astype(F32)).astype(BF16)


def product(left, right):
    left_high, left_low = left
    right_high, right_low = right
    dot = lambda p, q: jnp.dot(p, q, preferred_element_type=F32)
    return dot(left_high, right_high) + (dot(left_high, right_low) + dot(left_low, right_high))


def on_diagonal(count):
    row = lax.broadcasted_iota(jnp.int32, (count, count), 0)
    return row == lax.broadcasted_iota(jnp.int32, (count, count), 1)


def diagonals(total):
    parts = []
    for a in range(SIDE):
        tile = jnp.where(on_diagonal(TILE), total[tile_at(a, a)], 0.0)
        parts.append(jnp.sum(tile, axis=0, keepdims=True))
    return jnp.concatenate(parts + [jnp.zeros((DIAGONAL - SIDE, TILE), F32)], axis=0)


def inverse_root(covariance):
    diagonal = on_diagonal(BLOCK)
    shifted = covariance * (1.0 / TOKENS) + jnp.where(diagonal, DAMPING, 0.0)
    squares = jnp.sum(jnp.sum(shifted * shifted, axis=0, keepdims=True), axis=1, keepdims=True)
    frob = jnp.sqrt(squares)
    y = shifted * (1.0 / frob)
    y_halves = halves(y)
    s = product(y_halves, y_halves)
    tail = product(halves(s), halves(0.0625 * s - 0.5625 * y))
    z = jnp.where(diagonal, 2.25, 0.0) - 2.4375 * y + 1.6875 * s + tail
    return z * (1.0 / jnp.sqrt(frob))


def first_kernel(acts, grads, out, packed):
    total = gram(acts[...])
    pack(total, packed)
    high, low = halves(diagonals(total))
    ends = jnp.concatenate([high, low], axis=0)
    for peer in range(PEERS):
        for part in range(SIDE):
            column = peer * BLOCK + part * TILE
            out[peer, part * TILE : (part + 1) * TILE, :] = grads[:, column : column + TILE]
        share = packed[peer * SHARE : (peer + 1) * SHARE, :]
        out[peer, RAW : RAW + SHARE, :] = share.astype(BF16)
        out[peer, RAW + SHARE : FIRST, :] = ends


def second_kernel(got, out, packed, share):
    tokens = jnp.concatenate(
        [got[:, p * TILE : (p + 1) * TILE, :].reshape(PEERS * TILE, TILE) for p in range(SIDE)],
        axis=1,
    )
    grad_total = gram(tokens)
    pack(grad_total, packed)
    total = jnp.zeros((SHARE, TILE), F32)
    ends = jnp.zeros((2 * DIAGONAL, TILE), F32)
    for peer in range(PEERS):
        total += got[peer, RAW : RAW + SHARE, :].astype(F32)
        ends += got[peer, RAW + SHARE : FIRST, :].astype(F32)
    share[...] = total
    grad_ends = halves(diagonals(grad_total))
    act_ends = halves(ends[0:DIAGONAL] + ends[DIAGONAL:])
    both = jnp.concatenate([*grad_ends, *act_ends], axis=0)
    for peer in range(PEERS):
        high, low = halves(share[peer * PIECE : (peer + 1) * PIECE, :])
        out[peer, 0:SHARE, :] = packed[peer * SHARE : (peer + 1) * SHARE, :].astype(BF16)
        out[peer, SHARE:GATHER, :] = high
        out[peer, GATHER : GATHER + PIECE, :] = low
        out[peer, GATHER + PIECE : SECOND, :] = both


def sum_kernel(got, out, ends):
    total = got[0].astype(F32)
    for peer in range(1, PEERS):
        total += got[peer].astype(F32)
    share = total[0:SHARE].astype(BF16)
    piece = (total[SHARE:GATHER] + total[GATHER : GATHER + PIECE]).astype(BF16)
    for peer in range(PEERS):
        out[peer, 0:SHARE, :] = share
        out[peer, SHARE:GATHER, :] = piece
    both = total[GATHER + PIECE : SECOND]
    ends[0:DIAGONAL, :] = both[0:DIAGONAL] + both[DIAGONAL : 2 * DIAGONAL]
    ends[DIAGONAL:, :] = both[2 * DIAGONAL : 3 * DIAGONAL] + both[3 * DIAGONAL :]


def grad_root_kernel(got, ends, out, full, packed):
    for peer in range(PEERS):
        packed[peer * SHARE : (peer + 1) * SHARE, :] = got[peer, 0:SHARE, :]
    unpack(packed, full, ends[0:DIAGONAL, :])
    root = inverse_root(full[...])
    pack(root, packed)
    out[0:HALF, :] = packed[rows(lax.axis_index("yl"), HALF), :]
    root_ends = diagonals(root)
    out[HALF:, :] = jnp.concatenate([root_ends, root_ends], axis=0).astype(BF16)


def copies_kernel(got, out):
    for place in range(PEERS):
        piece = got[place, SHARE:GATHER, :]
        for peer in range(PEERS):
            out[peer, place * PIECE : (place + 1) * PIECE, :] = piece


def left_kernel(got, ends, grad, out, full):
    unpack(got, full, ends[DIAGONAL:, :])
    root = inverse_root(full[...]).astype(BF16)
    out[...] = jnp.dot(root, grad[...], preferred_element_type=F32).astype(BF16)


def last_kernel(left, mine, other, out, packed, full):
    bit = lax.axis_index("c")
    packed[rows(bit, HALF), :] = mine[0:HALF, :]
    packed[rows(1 - bit, HALF), :] = other[0:HALF, :]
    unpack(packed, full, mine[HALF:ROOT, :].astype(F32))
    out[...] = jnp.dot(left[...], full[...], preferred_element_type=F32)


def call(kernel, args, outs, scratch=(), flops=1 << 20, after=()):
    outs = [jax.ShapeDtypeStruct(dims, dtype) for dims, dtype in outs]
    data = sum(a.size * a.dtype.itemsize for a in [*args, *outs])

    def body(*refs):
        kernel(*refs[: len(args)], *refs[len(args) + len(after) :])

    got = pl.pallas_call(
        body,
        out_shape=outs,
        in_specs=[VMEM] * len(args) + [ANYWHERE] * len(after),
        out_specs=[VMEM] * len(outs),
        scratch_shapes=[pltpu.VMEM(dims, dtype) for dims, dtype in scratch],
        compiler_params=PARAMS,
        cost_estimate=pl.CostEstimate(flops=flops, bytes_accessed=data, transcendentals=0),
    )(*args, *after)
    return got if len(outs) > 1 else got[0]


def exchange(data, axes):
    return lax.all_to_all(data, axes, split_axis=0, concat_axis=0, tiled=True)


def swap(data, axis, size, distance):
    return lax.ppermute(data, axis, [(i, i ^ distance) for i in range(size)])


def transpose_places(data):
    places = np.arange(np.prod(SIZES)).reshape(SIZES)
    pairs = [
        (int(places[x, yl, z, yh, c]), int(places[yh, c, z, (x + yh) % 4, yl]))
        for x, yl, z, yh, c in np.ndindex(*SIZES)
    ]
    return lax.ppermute(data, AXES, pairs)


def on_device(acts, grads_out, grad):
    cube = 2 * BLOCK**3
    packed, full = (PACKED, TILE), (BLOCK, BLOCK)

    share = (SHARE, TILE)
    sent = call(
        first_kernel,
        [acts, grads_out],
        [((PEERS, FIRST, TILE), BF16)],
        [(packed, F32)],
        cube // 4,
    )
    got = exchange(sent, "z")
    sent = call(
        second_kernel,
        [got],
        [((PEERS, SECOND, TILE), BF16)],
        [(packed, F32), (share, F32)],
        2 * cube,
    )
    got = exchange(sent, ("x", "yl"))
    sent, ends = call(
        sum_kernel, [got], [((PEERS, GATHER, TILE), BF16), ((2 * DIAGONAL, TILE), F32)]
    )
    got = exchange(sent, ("x", "yl"))
    root = call(
        grad_root_kernel,
        [got, ends],
        [((ROOT, TILE), BF16)],
        [(full, F32), (packed, BF16)],
        6 * cube,
    )
    mine = transpose_places(root)
    sent = call(copies_kernel, [got], [((PEERS, SHARE, TILE), BF16)], after=[root])
    act_cov = exchange(sent, "z").reshape(packed)
    left = call(left_kernel, [act_cov, ends, grad], [(full, BF16)], [(full, F32)], 7 * cube)
    other = swap(mine, "c", 2, 1)
    return call(
        last_kernel, [left, mine, other], [(full, F32)], [(packed, BF16), (full, BF16)], cube
    )


def solution(mesh):
    split = Mesh(mesh.devices.reshape(SIZES), AXES)
    dp, tensor = AXES[:3], AXES[3:]
    return jax.shard_map(
        on_device,
        mesh=split,
        in_specs=(P(dp, tensor), P(dp, tensor), P(tensor, dp)),
        out_specs=P(tensor, dp),
        check_vma=False,
    )
```

```python
import jax
import jax.numpy as jnp
import numpy as np
from jax import lax
from jax.experimental import pallas as pl
from jax.experimental.pallas import tpu as pltpu
from jax.sharding import Mesh, PartitionSpec as P

TOKENS = 8192
DAMPING = 0.1
BLOCK = 512
TILE = 128
SIDE = BLOCK // TILE
UPPER = [(a, b) for a in range(SIDE) for b in range(a + 1, SIDE)]
PAIRS = range(0, SIDE, 2)
PACKED = (len(UPPER) + len(PAIRS)) * TILE
PEERS = 8
SHARE = PACKED // PEERS
PIECE = SHARE // PEERS
RAW = SIDE * TILE
DIAGONAL = 8
FIRST = RAW + SHARE + 2 * DIAGONAL
GATHER = SHARE + PIECE
SECOND = GATHER + PIECE + 4 * DIAGONAL
ROOT = PACKED + 2 * DIAGONAL
BF16, F32 = jnp.bfloat16, jnp.float32
AXES = ("x", "yl", "z", "yh", "c")
SIZES = (4, 2, 8, 4, 2)
VMEM = pl.BlockSpec(memory_space=pltpu.VMEM)
ANYWHERE = pl.BlockSpec(memory_space=pl.ANY)
PARAMS = pltpu.CompilerParams(vmem_limit_bytes=24 * 1024 * 1024)


def gram(data):
    return lax.dot_general(data, data, (((0,), (0,)), ((), ())), preferred_element_type=F32)


def tile_at(a, b):
    return slice(a * TILE, (a + 1) * TILE), slice(b * TILE, (b + 1) * TILE)


def over_diagonal():
    row = lax.broadcasted_iota(jnp.int32, (TILE, TILE), 0)
    return row < lax.broadcasted_iota(jnp.int32, (TILE, TILE), 1)


def pack(total, packed):
    tiles = [total[tile_at(a, b)] for a, b in UPPER]
    for a in PAIRS:
        first, second = total[tile_at(a, a)], total[tile_at(a + 1, a + 1)]
        tiles.append(jnp.where(over_diagonal(), first, second))
    for place, tile in enumerate(tiles):
        packed[place * TILE : (place + 1) * TILE, :] = tile.astype(packed.dtype)


def unpack(packed, full, ends):
    tiles = [packed[start : start + TILE, :].astype(F32) for start in range(0, PACKED, TILE)]
    for (a, b), tile in zip(UPPER, tiles):
        full[tile_at(a, b)] = tile.astype(full.dtype)
        full[tile_at(b, a)] = tile.T.astype(full.dtype)
    for a, tile in zip(PAIRS, tiles[len(UPPER) :]):
        turned = tile.T
        both = (tile, turned), (turned, tile)
        for place, (above, below) in enumerate(both, start=a):
            whole = jnp.where(over_diagonal(), above, below)
            whole = jnp.where(on_diagonal(TILE), ends[place : place + 1, :], whole)
            full[tile_at(place, place)] = whole.astype(full.dtype)


def halves(values):
    high = values.astype(BF16)
    return high, (values - high.astype(F32)).astype(BF16)


def product(left, right):
    left_high, left_low = left
    right_high, right_low = right
    dot = lambda p, q: jnp.dot(p, q, preferred_element_type=F32)
    return dot(left_high, right_high) + (dot(left_high, right_low) + dot(left_low, right_high))


def on_diagonal(count):
    row = lax.broadcasted_iota(jnp.int32, (count, count), 0)
    return row == lax.broadcasted_iota(jnp.int32, (count, count), 1)


def diagonals(total):
    parts = []
    for a in range(SIDE):
        tile = jnp.where(on_diagonal(TILE), total[tile_at(a, a)], 0.0)
        parts.append(jnp.sum(tile, axis=0, keepdims=True))
    return jnp.concatenate(parts + [jnp.zeros((DIAGONAL - SIDE, TILE), F32)], axis=0)


def inverse_root(covariance):
    diagonal = on_diagonal(BLOCK)
    shifted = covariance * (1.0 / TOKENS) + jnp.where(diagonal, DAMPING, 0.0)
    squares = jnp.sum(jnp.sum(shifted * shifted, axis=0, keepdims=True), axis=1, keepdims=True)
    frob = jnp.sqrt(squares)
    y = shifted * (1.0 / frob)
    y_halves = halves(y)
    s = product(y_halves, y_halves)
    tail = product(halves(s), halves(0.0625 * s - 0.5625 * y))
    z = jnp.where(diagonal, 2.25, 0.0) - 2.4375 * y + 1.6875 * s + tail
    return z * (1.0 / jnp.sqrt(frob))


def first_kernel(acts, grads, out, packed):
    total = gram(acts[...])
    pack(total, packed)
    high, low = halves(diagonals(total))
    ends = jnp.concatenate([high, low], axis=0)
    for peer in range(PEERS):
        for part in range(SIDE):
            column = peer * BLOCK + part * TILE
            out[peer, part * TILE : (part + 1) * TILE, :] = grads[:, column : column + TILE]
        share = packed[peer * SHARE : (peer + 1) * SHARE, :]
        out[peer, RAW : RAW + SHARE, :] = share.astype(BF16)
        out[peer, RAW + SHARE : FIRST, :] = ends


def second_kernel(got, out, packed, share):
    tokens = jnp.concatenate(
        [got[:, p * TILE : (p + 1) * TILE, :].reshape(PEERS * TILE, TILE) for p in range(SIDE)],
        axis=1,
    )
    grad_total = gram(tokens)
    pack(grad_total, packed)
    total = jnp.zeros((SHARE, TILE), F32)
    ends = jnp.zeros((2 * DIAGONAL, TILE), F32)
    for peer in range(PEERS):
        total += got[peer, RAW : RAW + SHARE, :].astype(F32)
        ends += got[peer, RAW + SHARE : FIRST, :].astype(F32)
    share[...] = total
    grad_ends = halves(diagonals(grad_total))
    act_ends = halves(ends[0:DIAGONAL] + ends[DIAGONAL:])
    both = jnp.concatenate([*grad_ends, *act_ends], axis=0)
    for peer in range(PEERS):
        high, low = halves(share[peer * PIECE : (peer + 1) * PIECE, :])
        out[peer, 0:SHARE, :] = packed[peer * SHARE : (peer + 1) * SHARE, :].astype(BF16)
        out[peer, SHARE:GATHER, :] = high
        out[peer, GATHER : GATHER + PIECE, :] = low
        out[peer, GATHER + PIECE : SECOND, :] = both


def sum_kernel(got, out, ends):
    total = got[0].astype(F32)
    for peer in range(1, PEERS):
        total += got[peer].astype(F32)
    share = total[0:SHARE].astype(BF16)
    piece = (total[SHARE:GATHER] + total[GATHER : GATHER + PIECE]).astype(BF16)
    for peer in range(PEERS):
        out[peer, 0:SHARE, :] = share
        out[peer, SHARE:GATHER, :] = piece
    both = total[GATHER + PIECE : SECOND]
    ends[0:DIAGONAL, :] = both[0:DIAGONAL] + both[DIAGONAL : 2 * DIAGONAL]
    ends[DIAGONAL:, :] = both[2 * DIAGONAL : 3 * DIAGONAL] + both[3 * DIAGONAL :]


def grad_root_kernel(got, ends, out, full, packed):
    for peer in range(PEERS):
        packed[peer * SHARE : (peer + 1) * SHARE, :] = got[peer, 0:SHARE, :]
    unpack(packed, full, ends[0:DIAGONAL, :])
    root = inverse_root(full[...])
    pack(root, out)
    root_ends = diagonals(root)
    out[PACKED:, :] = jnp.concatenate([root_ends, root_ends], axis=0).astype(BF16)


def copies_kernel(got, out):
    for place in range(PEERS):
        piece = got[place, SHARE:GATHER, :]
        for peer in range(PEERS):
            out[peer, place * PIECE : (place + 1) * PIECE, :] = piece


def left_kernel(got, ends, grad, out, full):
    unpack(got, full, ends[DIAGONAL:, :])
    root = inverse_root(full[...]).astype(BF16)
    out[...] = jnp.dot(root, grad[...], preferred_element_type=F32).astype(BF16)


def last_kernel(left, root, out, full):
    unpack(root, full, root[PACKED:, :].astype(F32))
    out[...] = jnp.dot(left[...], full[...], preferred_element_type=F32)


def call(kernel, args, outs, scratch=(), flops=1 << 20, after=()):
    outs = [jax.ShapeDtypeStruct(dims, dtype) for dims, dtype in outs]
    data = sum(a.size * a.dtype.itemsize for a in [*args, *outs])

    def body(*refs):
        kernel(*refs[: len(args)], *refs[len(args) + len(after) :])

    got = pl.pallas_call(
        body,
        out_shape=outs,
        in_specs=[VMEM] * len(args) + [ANYWHERE] * len(after),
        out_specs=[VMEM] * len(outs),
        scratch_shapes=[pltpu.VMEM(dims, dtype) for dims, dtype in scratch],
        compiler_params=PARAMS,
        cost_estimate=pl.CostEstimate(flops=flops, bytes_accessed=data, transcendentals=0),
    )(*args, *after)
    return got if len(outs) > 1 else got[0]


def exchange(data, axes):
    return lax.all_to_all(data, axes, split_axis=0, concat_axis=0, tiled=True)


def transpose_places(data):
    places = np.arange(np.prod(SIZES)).reshape(SIZES)
    pairs = [
        (int(places[x, yl, z, yh, c]), int(places[yh, c, z, (x + yh) % 4, yl]))
        for x, yl, z, yh, c in np.ndindex(*SIZES)
    ]
    return lax.ppermute(data, AXES, pairs)


def on_device(acts, grads_out, grad):
    cube = 2 * BLOCK**3
    packed, full = (PACKED, TILE), (BLOCK, BLOCK)

    share = (SHARE, TILE)
    sent = call(
        first_kernel,
        [acts, grads_out],
        [((PEERS, FIRST, TILE), BF16)],
        [(packed, F32)],
        cube // 4,
    )
    got = exchange(sent, "z")
    sent = call(
        second_kernel,
        [got],
        [((PEERS, SECOND, TILE), BF16)],
        [(packed, F32), (share, F32)],
        2 * cube,
    )
    got = exchange(sent, ("x", "yl"))
    sent, ends = call(
        sum_kernel, [got], [((PEERS, GATHER, TILE), BF16), ((2 * DIAGONAL, TILE), F32)]
    )
    got = exchange(sent, ("x", "yl"))
    root = call(
        grad_root_kernel,
        [got, ends],
        [((ROOT, TILE), BF16)],
        [(full, F32), (packed, BF16)],
        6 * cube,
    )
    grad_root = transpose_places(root)
    sent = call(copies_kernel, [got], [((PEERS, SHARE, TILE), BF16)], after=[root])
    act_cov = exchange(sent, "z").reshape(packed)
    left = call(left_kernel, [act_cov, ends, grad], [(full, BF16)], [(full, F32)], 7 * cube)
    return call(last_kernel, [left, grad_root], [(full, F32)], [(full, BF16)], cube)


def solution(mesh):
    split = Mesh(mesh.devices.reshape(SIZES), AXES)
    dp, tensor = AXES[:3], AXES[3:]
    return jax.shard_map(
        on_device,
        mesh=split,
        in_specs=(P(dp, tensor), P(dp, tensor), P(tensor, dp)),
        out_specs=P(tensor, dp),
        check_vma=False,
    )
```

```python
import jax
import jax.numpy as jnp
import numpy as np
from jax import lax
from jax.experimental import pallas as pl
from jax.experimental.pallas import tpu as pltpu
from jax.sharding import Mesh, PartitionSpec as P

TOKENS = 8192
DAMPING = 0.1
BLOCK = 512
TILE = 128
SIDE = BLOCK // TILE
UPPER = [(a, b) for a in range(SIDE) for b in range(a + 1, SIDE)]
PAIRS = range(0, SIDE, 2)
PACKED = (len(UPPER) + len(PAIRS)) * TILE
PEERS = 8
SHARE = PACKED // PEERS
PIECE = SHARE // PEERS
RAW = SIDE * TILE
DIAGONAL = 8
FIRST = RAW + SHARE + 2 * DIAGONAL
GATHER = SHARE + PIECE
SECOND = GATHER + PIECE + 4 * DIAGONAL
ROOT = PACKED + 2 * DIAGONAL
BF16, F32 = jnp.bfloat16, jnp.float32
AXES = ("x", "yl", "z", "yh", "c")
SIZES = (4, 2, 8, 4, 2)
VMEM = pl.BlockSpec(memory_space=pltpu.VMEM)
ANYWHERE = pl.BlockSpec(memory_space=pl.ANY)
PARAMS = pltpu.CompilerParams(vmem_limit_bytes=24 * 1024 * 1024)


def gram(data):
    return lax.dot_general(data, data, (((0,), (0,)), ((), ())), preferred_element_type=F32)


def tile_at(a, b):
    return slice(a * TILE, (a + 1) * TILE), slice(b * TILE, (b + 1) * TILE)


def over_diagonal():
    row = lax.broadcasted_iota(jnp.int32, (TILE, TILE), 0)
    return row < lax.broadcasted_iota(jnp.int32, (TILE, TILE), 1)


def pack(total, packed):
    tiles = [total[tile_at(a, b)] for a, b in UPPER]
    for a in PAIRS:
        first, second = total[tile_at(a, a)], total[tile_at(a + 1, a + 1)]
        tiles.append(jnp.where(over_diagonal(), first, second))
    for place, tile in enumerate(tiles):
        packed[place * TILE : (place + 1) * TILE, :] = tile.astype(packed.dtype)


def unpack(packed, full, ends):
    tiles = [packed[start : start + TILE, :].astype(F32) for start in range(0, PACKED, TILE)]
    for (a, b), tile in zip(UPPER, tiles):
        full[tile_at(a, b)] = tile.astype(full.dtype)
        full[tile_at(b, a)] = tile.T.astype(full.dtype)
    for a, tile in zip(PAIRS, tiles[len(UPPER) :]):
        turned = tile.T
        both = (tile, turned), (turned, tile)
        for place, (above, below) in enumerate(both, start=a):
            whole = jnp.where(over_diagonal(), above, below)
            whole = jnp.where(on_diagonal(TILE), ends[place : place + 1, :], whole)
            full[tile_at(place, place)] = whole.astype(full.dtype)


def halves(values):
    high = values.astype(BF16)
    return high, (values - high.astype(F32)).astype(BF16)


def product(left, right):
    left_high, left_low = left
    right_high, right_low = right
    dot = lambda p, q: jnp.dot(p, q, preferred_element_type=F32)
    return dot(left_high, right_high) + (dot(left_high, right_low) + dot(left_low, right_high))


def on_diagonal(count):
    row = lax.broadcasted_iota(jnp.int32, (count, count), 0)
    return row == lax.broadcasted_iota(jnp.int32, (count, count), 1)


def diagonals(total):
    parts = []
    for a in range(SIDE):
        tile = jnp.where(on_diagonal(TILE), total[tile_at(a, a)], 0.0)
        parts.append(jnp.sum(tile, axis=0, keepdims=True))
    return jnp.concatenate(parts + [jnp.zeros((DIAGONAL - SIDE, TILE), F32)], axis=0)


def inverse_root(covariance):
    diagonal = on_diagonal(BLOCK)
    shifted = covariance * (1.0 / TOKENS) + jnp.where(diagonal, DAMPING, 0.0)
    squares = jnp.sum(jnp.sum(shifted * shifted, axis=0, keepdims=True), axis=1, keepdims=True)
    frob = jnp.sqrt(squares)
    y = shifted * (1.0 / frob)
    y_halves = halves(y)
    s = product(y_halves, y_halves)
    tail = product(halves(s), halves(0.0625 * s - 0.5625 * y))
    z = jnp.where(diagonal, 2.25, 0.0) - 2.4375 * y + 1.6875 * s + tail
    return z * (1.0 / jnp.sqrt(frob))


def first_kernel(acts, grads, out, packed):
    total = gram(acts[...])
    pack(total, packed)
    high, low = halves(diagonals(total))
    ends = jnp.concatenate([high, low], axis=0)
    for peer in range(PEERS):
        for part in range(SIDE):
            column = peer * BLOCK + part * TILE
            out[peer, part * TILE : (part + 1) * TILE, :] = grads[:, column : column + TILE]
        share = packed[peer * SHARE : (peer + 1) * SHARE, :]
        out[peer, RAW : RAW + SHARE, :] = share.astype(BF16)
        out[peer, RAW + SHARE : FIRST, :] = ends


def second_kernel(got, out, packed, share):
    tokens = jnp.concatenate(
        [got[:, p * TILE : (p + 1) * TILE, :].reshape(PEERS * TILE, TILE) for p in range(SIDE)],
        axis=1,
    )
    grad_total = gram(tokens)
    pack(grad_total, packed)
    total = jnp.zeros((SHARE, TILE), F32)
    ends = jnp.zeros((2 * DIAGONAL, TILE), F32)
    for peer in range(PEERS):
        total += got[peer, RAW : RAW + SHARE, :].astype(F32)
        ends += got[peer, RAW + SHARE : FIRST, :].astype(F32)
    share[...] = total
    grad_ends = halves(diagonals(grad_total))
    act_ends = halves(ends[0:DIAGONAL] + ends[DIAGONAL:])
    both = jnp.concatenate([*grad_ends, *act_ends], axis=0)
    for peer in range(PEERS):
        high, low = halves(share[peer * PIECE : (peer + 1) * PIECE, :])
        out[peer, 0:SHARE, :] = packed[peer * SHARE : (peer + 1) * SHARE, :].astype(BF16)
        out[peer, SHARE:GATHER, :] = high
        out[peer, GATHER : GATHER + PIECE, :] = low
        out[peer, GATHER + PIECE : SECOND, :] = both


def sum_kernel(got, out, ends):
    total = got[0].astype(F32)
    for peer in range(1, PEERS):
        total += got[peer].astype(F32)
    share = total[0:SHARE].astype(BF16)
    piece = (total[SHARE:GATHER] + total[GATHER : GATHER + PIECE]).astype(BF16)
    for peer in range(PEERS):
        out[peer, 0:SHARE, :] = share
        out[peer, SHARE:GATHER, :] = piece
    both = total[GATHER + PIECE : SECOND]
    ends[0:DIAGONAL, :] = both[0:DIAGONAL] + both[DIAGONAL : 2 * DIAGONAL]
    ends[DIAGONAL:, :] = both[2 * DIAGONAL : 3 * DIAGONAL] + both[3 * DIAGONAL :]


def grad_root_kernel(got, ends, out, full, packed):
    for peer in range(PEERS):
        packed[peer * SHARE : (peer + 1) * SHARE, :] = got[peer, 0:SHARE, :]
    unpack(packed, full, ends[0:DIAGONAL, :])
    root = inverse_root(full[...])
    pack(root, out)
    root_ends = diagonals(root)
    out[PACKED:, :] = jnp.concatenate([root_ends, root_ends], axis=0).astype(BF16)


def copies_kernel(got, out):
    for place in range(PEERS):
        piece = got[place, SHARE:GATHER, :]
        for peer in range(PEERS):
            out[peer, place * PIECE : (place + 1) * PIECE, :] = piece


def unpack_kernel(root, out):
    unpack(root, out, root[PACKED:, :].astype(F32))


def left_kernel(got, ends, grad, out, full):
    unpack(got, full, ends[DIAGONAL:, :])
    root = inverse_root(full[...]).astype(BF16)
    out[...] = jnp.dot(root, grad[...], preferred_element_type=F32).astype(BF16)


def last_kernel(left, root, out):
    out[...] = jnp.dot(left[...], root[...], preferred_element_type=F32)


def call(kernel, args, outs, scratch=(), flops=1 << 20, after=()):
    outs = [jax.ShapeDtypeStruct(dims, dtype) for dims, dtype in outs]
    data = sum(a.size * a.dtype.itemsize for a in [*args, *outs])

    def body(*refs):
        kernel(*refs[: len(args)], *refs[len(args) + len(after) :])

    got = pl.pallas_call(
        body,
        out_shape=outs,
        in_specs=[VMEM] * len(args) + [ANYWHERE] * len(after),
        out_specs=[VMEM] * len(outs),
        scratch_shapes=[pltpu.VMEM(dims, dtype) for dims, dtype in scratch],
        compiler_params=PARAMS,
        cost_estimate=pl.CostEstimate(flops=flops, bytes_accessed=data, transcendentals=0),
    )(*args, *after)
    return got if len(outs) > 1 else got[0]


def exchange(data, axes):
    return lax.all_to_all(data, axes, split_axis=0, concat_axis=0, tiled=True)


def transpose_places(data):
    places = np.arange(np.prod(SIZES)).reshape(SIZES)
    pairs = [
        (int(places[x, yl, z, yh, c]), int(places[yh, c, z, (x + yh) % 4, yl]))
        for x, yl, z, yh, c in np.ndindex(*SIZES)
    ]
    return lax.ppermute(data, AXES, pairs)


def on_device(acts, grads_out, grad):
    cube = 2 * BLOCK**3
    packed, full = (PACKED, TILE), (BLOCK, BLOCK)

    share = (SHARE, TILE)
    sent = call(
        first_kernel,
        [acts, grads_out],
        [((PEERS, FIRST, TILE), BF16)],
        [(packed, F32)],
        cube // 4,
    )
    got = exchange(sent, "z")
    sent = call(
        second_kernel,
        [got],
        [((PEERS, SECOND, TILE), BF16)],
        [(packed, F32), (share, F32)],
        2 * cube,
    )
    got = exchange(sent, ("x", "yl"))
    sent, ends = call(
        sum_kernel, [got], [((PEERS, GATHER, TILE), BF16), ((2 * DIAGONAL, TILE), F32)]
    )
    got = exchange(sent, ("x", "yl"))
    root = call(
        grad_root_kernel,
        [got, ends],
        [((ROOT, TILE), BF16)],
        [(full, F32), (packed, BF16)],
        6 * cube,
    )
    grad_root = transpose_places(root)
    sent = call(copies_kernel, [got], [((PEERS, SHARE, TILE), BF16)], after=[root])
    act_cov = exchange(sent, "z").reshape(packed)
    grad_root = call(unpack_kernel, [grad_root], [(full, BF16)], (), 14 * cube)
    left = call(
        left_kernel, [act_cov, ends, grad], [(full, BF16)], [(full, F32)], 7 * cube, [grad_root]
    )
    return call(last_kernel, [left, grad_root], [(full, F32)], (), cube)


def solution(mesh):
    split = Mesh(mesh.devices.reshape(SIZES), AXES)
    dp, tensor = AXES[:3], AXES[3:]
    return jax.shard_map(
        on_device,
        mesh=split,
        in_specs=(P(dp, tensor), P(dp, tensor), P(tensor, dp)),
        out_specs=P(tensor, dp),
        check_vma=False,
    )
```

```python
import jax
import jax.numpy as jnp
import numpy as np
from jax import lax
from jax.experimental import pallas as pl
from jax.experimental.pallas import tpu as pltpu
from jax.sharding import Mesh, PartitionSpec as P

TOKENS = 8192
DAMPING = 0.1
BLOCK = 512
TILE = 128
SIDE = BLOCK // TILE
UPPER = [(a, b) for a in range(SIDE) for b in range(a + 1, SIDE)]
PAIRS = range(0, SIDE, 2)
PACKED = (len(UPPER) + len(PAIRS)) * TILE
HALF = PACKED // 2
PEERS = 8
SHARE = PACKED // PEERS
PIECE = SHARE // PEERS
RAW = SIDE * TILE
DIAGONAL = 8
FIRST = RAW + SHARE + 2 * DIAGONAL
GATHER = SHARE + PIECE
SECOND = GATHER + PIECE + 4 * DIAGONAL
ROOT = HALF + 2 * DIAGONAL
BF16, F32 = jnp.bfloat16, jnp.float32
AXES = ("x", "yl", "z", "yh", "c")
SIZES = (4, 2, 8, 4, 2)
VMEM = pl.BlockSpec(memory_space=pltpu.VMEM)
ANYWHERE = pl.BlockSpec(memory_space=pl.ANY)
PARAMS = pltpu.CompilerParams(vmem_limit_bytes=24 * 1024 * 1024)


def gram(data):
    return lax.dot_general(data, data, (((0,), (0,)), ((), ())), preferred_element_type=F32)


def tile_at(a, b):
    return slice(a * TILE, (a + 1) * TILE), slice(b * TILE, (b + 1) * TILE)


def over_diagonal():
    row = lax.broadcasted_iota(jnp.int32, (TILE, TILE), 0)
    return row < lax.broadcasted_iota(jnp.int32, (TILE, TILE), 1)


def pack(total, packed):
    tiles = [total[tile_at(a, b)] for a, b in UPPER]
    for a in PAIRS:
        first, second = total[tile_at(a, a)], total[tile_at(a + 1, a + 1)]
        tiles.append(jnp.where(over_diagonal(), first, second))
    for place, tile in enumerate(tiles):
        packed[place * TILE : (place + 1) * TILE, :] = tile.astype(packed.dtype)


def unpack(packed, full, ends):
    tiles = [packed[start : start + TILE, :].astype(F32) for start in range(0, PACKED, TILE)]
    for (a, b), tile in zip(UPPER, tiles):
        full[tile_at(a, b)] = tile.astype(full.dtype)
        full[tile_at(b, a)] = tile.T.astype(full.dtype)
    for a, tile in zip(PAIRS, tiles[len(UPPER) :]):
        turned = tile.T
        both = (tile, turned), (turned, tile)
        for place, (above, below) in enumerate(both, start=a):
            whole = jnp.where(over_diagonal(), above, below)
            whole = jnp.where(on_diagonal(TILE), ends[place : place + 1, :], whole)
            full[tile_at(place, place)] = whole.astype(full.dtype)


def rows(bit, count):
    return pl.ds(pl.multiple_of(bit * count, count), count)


def halves(values):
    high = values.astype(BF16)
    return high, (values - high.astype(F32)).astype(BF16)


def product(left, right):
    left_high, left_low = left
    right_high, right_low = right
    dot = lambda p, q: jnp.dot(p, q, preferred_element_type=F32)
    return dot(left_high, right_high) + (dot(left_high, right_low) + dot(left_low, right_high))


def on_diagonal(count):
    row = lax.broadcasted_iota(jnp.int32, (count, count), 0)
    return row == lax.broadcasted_iota(jnp.int32, (count, count), 1)


def diagonals(total):
    parts = []
    for a in range(SIDE):
        tile = jnp.where(on_diagonal(TILE), total[tile_at(a, a)], 0.0)
        parts.append(jnp.sum(tile, axis=0, keepdims=True))
    return jnp.concatenate(parts + [jnp.zeros((DIAGONAL - SIDE, TILE), F32)], axis=0)


def inverse_root(covariance):
    diagonal = on_diagonal(BLOCK)
    shifted = covariance * (1.0 / TOKENS) + jnp.where(diagonal, DAMPING, 0.0)
    squares = jnp.sum(jnp.sum(shifted * shifted, axis=0, keepdims=True), axis=1, keepdims=True)
    frob = jnp.sqrt(squares)
    y = shifted * (1.0 / frob)
    y_halves = halves(y)
    s = product(y_halves, y_halves)
    tail = product(halves(s), halves(0.0625 * s - 0.5625 * y))
    z = jnp.where(diagonal, 2.25, 0.0) - 2.4375 * y + 1.6875 * s + tail
    return z * (1.0 / jnp.sqrt(frob))


def first_kernel(acts, grads, out, packed):
    total = gram(acts[...])
    pack(total, packed)
    high, low = halves(diagonals(total))
    ends = jnp.concatenate([high, low], axis=0)
    for peer in range(PEERS):
        for part in range(SIDE):
            column = peer * BLOCK + part * TILE
            out[peer, part * TILE : (part + 1) * TILE, :] = grads[:, column : column + TILE]
        share = packed[peer * SHARE : (peer + 1) * SHARE, :]
        out[peer, RAW : RAW + SHARE, :] = share.astype(BF16)
        out[peer, RAW + SHARE : FIRST, :] = ends


def second_kernel(got, out, packed, share):
    tokens = jnp.concatenate(
        [got[:, p * TILE : (p + 1) * TILE, :].reshape(PEERS * TILE, TILE) for p in range(SIDE)],
        axis=1,
    )
    grad_total = gram(tokens)
    pack(grad_total, packed)
    total = jnp.zeros((SHARE, TILE), F32)
    ends = jnp.zeros((2 * DIAGONAL, TILE), F32)
    for peer in range(PEERS):
        total += got[peer, RAW : RAW + SHARE, :].astype(F32)
        ends += got[peer, RAW + SHARE : FIRST, :].astype(F32)
    share[...] = total
    grad_ends = halves(diagonals(grad_total))
    act_ends = halves(ends[0:DIAGONAL] + ends[DIAGONAL:])
    both = jnp.concatenate([*grad_ends, *act_ends], axis=0)
    for peer in range(PEERS):
        high, low = halves(share[peer * PIECE : (peer + 1) * PIECE, :])
        out[peer, 0:SHARE, :] = packed[peer * SHARE : (peer + 1) * SHARE, :].astype(BF16)
        out[peer, SHARE:GATHER, :] = high
        out[peer, GATHER : GATHER + PIECE, :] = low
        out[peer, GATHER + PIECE : SECOND, :] = both


def sum_kernel(got, out, ends):
    total = got[0].astype(F32)
    for peer in range(1, PEERS):
        total += got[peer].astype(F32)
    share = total[0:SHARE].astype(BF16)
    piece = (total[SHARE:GATHER] + total[GATHER : GATHER + PIECE]).astype(BF16)
    for peer in range(PEERS):
        out[peer, 0:SHARE, :] = share
        out[peer, SHARE:GATHER, :] = piece
    both = total[GATHER + PIECE : SECOND]
    ends[0:DIAGONAL, :] = both[0:DIAGONAL] + both[DIAGONAL : 2 * DIAGONAL]
    ends[DIAGONAL:, :] = both[2 * DIAGONAL : 3 * DIAGONAL] + both[3 * DIAGONAL :]


def grad_root_kernel(got, ends, out, full, packed):
    for peer in range(PEERS):
        packed[peer * SHARE : (peer + 1) * SHARE, :] = got[peer, 0:SHARE, :]
    unpack(packed, full, ends[0:DIAGONAL, :])
    root = inverse_root(full[...])
    pack(root, packed)
    out[0:HALF, :] = packed[rows(lax.axis_index("yl"), HALF), :]
    root_ends = diagonals(root)
    out[HALF:, :] = jnp.concatenate([root_ends, root_ends], axis=0).astype(BF16)


def copies_kernel(got, out):
    for place in range(PEERS):
        piece = got[place, SHARE:GATHER, :]
        for peer in range(PEERS):
            out[peer, place * PIECE : (place + 1) * PIECE, :] = piece


def left_kernel(got, ends, grad, out, full):
    unpack(got, full, ends[DIAGONAL:, :])
    root = inverse_root(full[...]).astype(BF16)
    out[...] = jnp.dot(root, grad[...], preferred_element_type=F32).astype(BF16)


def keep_kernel(got, out):
    out[...] = got[...]


def last_kernel(left, mine, other, out, packed, full):
    bit = lax.axis_index("c")
    packed[rows(bit, HALF), :] = mine[0:HALF, :]
    packed[rows(1 - bit, HALF), :] = other[0:HALF, :]
    unpack(packed, full, mine[HALF:ROOT, :].astype(F32))
    out[...] = jnp.dot(left[...], full[...], preferred_element_type=F32)


def call(kernel, args, outs, scratch=(), flops=1 << 20, after=()):
    outs = [jax.ShapeDtypeStruct(dims, dtype) for dims, dtype in outs]
    data = sum(a.size * a.dtype.itemsize for a in [*args, *outs])

    def body(*refs):
        kernel(*refs[: len(args)], *refs[len(args) + len(after) :])

    got = pl.pallas_call(
        body,
        out_shape=outs,
        in_specs=[VMEM] * len(args) + [ANYWHERE] * len(after),
        out_specs=[VMEM] * len(outs),
        scratch_shapes=[pltpu.VMEM(dims, dtype) for dims, dtype in scratch],
        compiler_params=PARAMS,
        cost_estimate=pl.CostEstimate(flops=flops, bytes_accessed=data, transcendentals=0),
    )(*args, *after)
    return got if len(outs) > 1 else got[0]


def exchange(data, axes):
    return lax.all_to_all(data, axes, split_axis=0, concat_axis=0, tiled=True)


def swap(data, axis, size, distance):
    return lax.ppermute(data, axis, [(i, i ^ distance) for i in range(size)])


def transpose_places(data):
    places = np.arange(np.prod(SIZES)).reshape(SIZES)
    pairs = [
        (int(places[x, yl, z, yh, c]), int(places[yh, c, z, (x + yh) % 4, yl]))
        for x, yl, z, yh, c in np.ndindex(*SIZES)
    ]
    return lax.ppermute(data, AXES, pairs)


def on_device(acts, grads_out, grad):
    cube = 2 * BLOCK**3
    packed, full = (PACKED, TILE), (BLOCK, BLOCK)

    share = (SHARE, TILE)
    sent = call(
        first_kernel,
        [acts, grads_out],
        [((PEERS, FIRST, TILE), BF16)],
        [(packed, F32)],
        cube // 4,
    )
    got = exchange(sent, "z")
    sent = call(
        second_kernel,
        [got],
        [((PEERS, SECOND, TILE), BF16)],
        [(packed, F32), (share, F32)],
        2 * cube,
    )
    got = exchange(sent, ("x", "yl"))
    sent, ends = call(
        sum_kernel, [got], [((PEERS, GATHER, TILE), BF16), ((2 * DIAGONAL, TILE), F32)]
    )
    got = exchange(sent, ("x", "yl"))
    root = call(
        grad_root_kernel,
        [got, ends],
        [((ROOT, TILE), BF16)],
        [(full, F32), (packed, BF16)],
        6 * cube,
    )
    mine = transpose_places(root)
    sent = call(copies_kernel, [got], [((PEERS, SHARE, TILE), BF16)], after=[root])
    act_cov = exchange(sent, "z").reshape(packed)
    left = call(left_kernel, [act_cov, ends, grad], [(full, BF16)], [(full, F32)], 7 * cube)
    kept = call(keep_kernel, [mine], [((ROOT, TILE), BF16)], after=[left])
    other = swap(kept, "c", 2, 1)
    return call(
        last_kernel, [left, mine, other], [(full, F32)], [(packed, BF16), (full, BF16)], cube
    )


def solution(mesh):
    split = Mesh(mesh.devices.reshape(SIZES), AXES)
    dp, tensor = AXES[:3], AXES[3:]
    return jax.shard_map(
        on_device,
        mesh=split,
        in_specs=(P(dp, tensor), P(dp, tensor), P(tensor, dp)),
        out_specs=P(tensor, dp),
        check_vma=False,
    )
```

```python
import jax
import jax.numpy as jnp
import numpy as np
from jax import lax
from jax.experimental import pallas as pl
from jax.experimental.pallas import tpu as pltpu
from jax.sharding import Mesh, PartitionSpec as P

TOKENS = 8192
DAMPING = 0.1
BLOCK = 512
TILE = 128
SIDE = BLOCK // TILE
UPPER = [(a, b) for a in range(SIDE) for b in range(a + 1, SIDE)]
PAIRS = range(0, SIDE, 2)
PACKED = (len(UPPER) + len(PAIRS)) * TILE
HALF = PACKED // 2
PEERS = 8
SHARE = PACKED // PEERS
PIECE = SHARE // PEERS
RAW = SIDE * TILE
DIAGONAL = 8
FIRST = RAW + SHARE + 2 * DIAGONAL
GATHER = SHARE + PIECE
SECOND = GATHER + PIECE + 4 * DIAGONAL
ROOT = HALF + 2 * DIAGONAL
BF16, F32 = jnp.bfloat16, jnp.float32
AXES = ("x", "yl", "z", "yh", "c")
SIZES = (4, 2, 8, 4, 2)
VMEM = pl.BlockSpec(memory_space=pltpu.VMEM)
ANYWHERE = pl.BlockSpec(memory_space=pl.ANY)
PARAMS = pltpu.CompilerParams(vmem_limit_bytes=24 * 1024 * 1024)


def gram(data):
    return lax.dot_general(data, data, (((0,), (0,)), ((), ())), preferred_element_type=F32)


def tile_at(a, b):
    return slice(a * TILE, (a + 1) * TILE), slice(b * TILE, (b + 1) * TILE)


def over_diagonal():
    row = lax.broadcasted_iota(jnp.int32, (TILE, TILE), 0)
    return row < lax.broadcasted_iota(jnp.int32, (TILE, TILE), 1)


def pack(total, packed):
    tiles = [total[tile_at(a, b)] for a, b in UPPER]
    for a in PAIRS:
        first, second = total[tile_at(a, a)], total[tile_at(a + 1, a + 1)]
        tiles.append(jnp.where(over_diagonal(), first, second))
    for place, tile in enumerate(tiles):
        packed[place * TILE : (place + 1) * TILE, :] = tile.astype(packed.dtype)


def unpack(packed, full, ends):
    tiles = [packed[start : start + TILE, :].astype(F32) for start in range(0, PACKED, TILE)]
    for (a, b), tile in zip(UPPER, tiles):
        full[tile_at(a, b)] = tile.astype(full.dtype)
        full[tile_at(b, a)] = tile.T.astype(full.dtype)
    for a, tile in zip(PAIRS, tiles[len(UPPER) :]):
        turned = tile.T
        both = (tile, turned), (turned, tile)
        for place, (above, below) in enumerate(both, start=a):
            whole = jnp.where(over_diagonal(), above, below)
            whole = jnp.where(on_diagonal(TILE), ends[place : place + 1, :], whole)
            full[tile_at(place, place)] = whole.astype(full.dtype)


def rows(bit, count):
    return pl.ds(pl.multiple_of(bit * count, count), count)


def halves(values):
    high = values.astype(BF16)
    return high, (values - high.astype(F32)).astype(BF16)


def product(left, right):
    left_high, left_low = left
    right_high, right_low = right
    dot = lambda p, q: jnp.dot(p, q, preferred_element_type=F32)
    return dot(left_high, right_high) + (dot(left_high, right_low) + dot(left_low, right_high))


def on_diagonal(count):
    row = lax.broadcasted_iota(jnp.int32, (count, count), 0)
    return row == lax.broadcasted_iota(jnp.int32, (count, count), 1)


def diagonals(total):
    parts = []
    for a in range(SIDE):
        tile = jnp.where(on_diagonal(TILE), total[tile_at(a, a)], 0.0)
        parts.append(jnp.sum(tile, axis=0, keepdims=True))
    return jnp.concatenate(parts + [jnp.zeros((DIAGONAL - SIDE, TILE), F32)], axis=0)


def inverse_root(covariance):
    diagonal = on_diagonal(BLOCK)
    shifted = covariance * (1.0 / TOKENS) + jnp.where(diagonal, DAMPING, 0.0)
    squares = jnp.sum(jnp.sum(shifted * shifted, axis=0, keepdims=True), axis=1, keepdims=True)
    frob = jnp.sqrt(squares)
    y = shifted * (1.0 / frob)
    y_halves = halves(y)
    s = product(y_halves, y_halves)
    tail = product(halves(s), halves(0.0625 * s - 0.5625 * y))
    z = jnp.where(diagonal, 2.25, 0.0) - 2.4375 * y + 1.6875 * s + tail
    return z * (1.0 / jnp.sqrt(frob))


def first_kernel(acts, grads, out, packed):
    total = gram(acts[...])
    pack(total, packed)
    high, low = halves(diagonals(total))
    ends = jnp.concatenate([high, low], axis=0)
    for peer in range(PEERS):
        for part in range(SIDE):
            column = peer * BLOCK + part * TILE
            out[peer, part * TILE : (part + 1) * TILE, :] = grads[:, column : column + TILE]
        share = packed[peer * SHARE : (peer + 1) * SHARE, :]
        out[peer, RAW : RAW + SHARE, :] = share.astype(BF16)
        out[peer, RAW + SHARE : FIRST, :] = ends


def second_kernel(got, out, packed, share):
    tokens = jnp.concatenate(
        [got[:, p * TILE : (p + 1) * TILE, :].reshape(PEERS * TILE, TILE) for p in range(SIDE)],
        axis=1,
    )
    grad_total = gram(tokens)
    pack(grad_total, packed)
    total = jnp.zeros((SHARE, TILE), F32)
    ends = jnp.zeros((2 * DIAGONAL, TILE), F32)
    for peer in range(PEERS):
        total += got[peer, RAW : RAW + SHARE, :].astype(F32)
        ends += got[peer, RAW + SHARE : FIRST, :].astype(F32)
    share[...] = total
    grad_ends = halves(diagonals(grad_total))
    act_ends = halves(ends[0:DIAGONAL] + ends[DIAGONAL:])
    both = jnp.concatenate([*grad_ends, *act_ends], axis=0)
    for peer in range(PEERS):
        high, low = halves(share[peer * PIECE : (peer + 1) * PIECE, :])
        out[peer, 0:SHARE, :] = packed[peer * SHARE : (peer + 1) * SHARE, :].astype(BF16)
        out[peer, SHARE:GATHER, :] = high
        out[peer, GATHER : GATHER + PIECE, :] = low
        out[peer, GATHER + PIECE : SECOND, :] = both


def sum_kernel(got, out, ends):
    total = got[0].astype(F32)
    for peer in range(1, PEERS):
        total += got[peer].astype(F32)
    share = total[0:SHARE].astype(BF16)
    piece = (total[SHARE:GATHER] + total[GATHER : GATHER + PIECE]).astype(BF16)
    for peer in range(PEERS):
        out[peer, 0:SHARE, :] = share
        out[peer, SHARE:GATHER, :] = piece
    both = total[GATHER + PIECE : SECOND]
    ends[0:DIAGONAL, :] = both[0:DIAGONAL] + both[DIAGONAL : 2 * DIAGONAL]
    ends[DIAGONAL:, :] = both[2 * DIAGONAL : 3 * DIAGONAL] + both[3 * DIAGONAL :]


def grad_root_kernel(got, ends, out, full, packed):
    for peer in range(PEERS):
        packed[peer * SHARE : (peer + 1) * SHARE, :] = got[peer, 0:SHARE, :]
    unpack(packed, full, ends[0:DIAGONAL, :])
    root = inverse_root(full[...])
    pack(root, packed)
    out[0:HALF, :] = packed[rows(lax.axis_index("yl"), HALF), :]
    root_ends = diagonals(root)
    out[HALF:, :] = jnp.concatenate([root_ends, root_ends], axis=0).astype(BF16)


def copies_kernel(got, out):
    for place in range(PEERS):
        piece = got[place, SHARE:GATHER, :]
        for peer in range(PEERS):
            out[peer, place * PIECE : (place + 1) * PIECE, :] = piece


def left_kernel(got, ends, grad, out, full):
    unpack(got, full, ends[DIAGONAL:, :])
    root = inverse_root(full[...]).astype(BF16)
    out[...] = jnp.dot(root, grad[...], preferred_element_type=F32).astype(BF16)


def keep_kernel(got, out):
    out[...] = got[...]


def last_kernel(left, mine, other, out, packed, full):
    bit = lax.axis_index("c")
    packed[rows(bit, HALF), :] = mine[0:HALF, :]
    packed[rows(1 - bit, HALF), :] = other[0:HALF, :]
    unpack(packed, full, mine[HALF:ROOT, :].astype(F32))
    out[...] = jnp.dot(left[...], full[...], preferred_element_type=F32)


def call(kernel, args, outs, scratch=(), flops=1 << 20, after=()):
    outs = [jax.ShapeDtypeStruct(dims, dtype) for dims, dtype in outs]
    data = sum(a.size * a.dtype.itemsize for a in [*args, *outs])

    def body(*refs):
        kernel(*refs[: len(args)], *refs[len(args) + len(after) :])

    got = pl.pallas_call(
        body,
        out_shape=outs,
        in_specs=[VMEM] * len(args) + [ANYWHERE] * len(after),
        out_specs=[VMEM] * len(outs),
        scratch_shapes=[pltpu.VMEM(dims, dtype) for dims, dtype in scratch],
        compiler_params=PARAMS,
        cost_estimate=pl.CostEstimate(flops=flops, bytes_accessed=data, transcendentals=0),
    )(*args, *after)
    return got if len(outs) > 1 else got[0]


def exchange(data, axes):
    return lax.all_to_all(data, axes, split_axis=0, concat_axis=0, tiled=True)


def swap(data, axis, size, distance):
    return lax.ppermute(data, axis, [(i, i ^ distance) for i in range(size)])


def transpose_places(data):
    places = np.arange(np.prod(SIZES)).reshape(SIZES)
    pairs = [
        (int(places[x, yl, z, yh, c]), int(places[yh, c, z, (x + yh) % 4, yl]))
        for x, yl, z, yh, c in np.ndindex(*SIZES)
    ]
    return lax.ppermute(data, AXES, pairs)


def on_device(acts, grads_out, grad):
    cube = 2 * BLOCK**3
    packed, full = (PACKED, TILE), (BLOCK, BLOCK)

    share = (SHARE, TILE)
    sent = call(
        first_kernel,
        [acts, grads_out],
        [((PEERS, FIRST, TILE), BF16)],
        [(packed, F32)],
        cube // 4,
    )
    got = exchange(sent, "z")
    sent = call(
        second_kernel,
        [got],
        [((PEERS, SECOND, TILE), BF16)],
        [(packed, F32), (share, F32)],
        2 * cube,
    )
    got = exchange(sent, ("x", "yl"))
    sent, ends = call(
        sum_kernel, [got], [((PEERS, GATHER, TILE), BF16), ((2 * DIAGONAL, TILE), F32)]
    )
    got = exchange(sent, ("x", "yl"))
    sent = call(copies_kernel, [got], [((PEERS, SHARE, TILE), BF16)])
    root = call(
        grad_root_kernel,
        [got, ends],
        [((ROOT, TILE), BF16)],
        [(full, F32), (packed, BF16)],
        6 * cube,
        [sent],
    )
    mine = transpose_places(root)
    act_cov = exchange(sent, "z").reshape(packed)
    left = call(left_kernel, [act_cov, ends, grad], [(full, BF16)], [(full, F32)], 7 * cube)
    kept = call(keep_kernel, [mine], [((ROOT, TILE), BF16)], after=[left])
    other = swap(kept, "c", 2, 1)
    return call(
        last_kernel, [left, mine, other], [(full, F32)], [(packed, BF16), (full, BF16)], cube
    )


def solution(mesh):
    split = Mesh(mesh.devices.reshape(SIZES), AXES)
    dp, tensor = AXES[:3], AXES[3:]
    return jax.shard_map(
        on_device,
        mesh=split,
        in_specs=(P(dp, tensor), P(dp, tensor), P(tensor, dp)),
        out_specs=P(tensor, dp),
        check_vma=False,
    )
```

```python
import jax
import jax.numpy as jnp
import numpy as np
from jax import lax
from jax.experimental import pallas as pl
from jax.experimental.pallas import tpu as pltpu
from jax.sharding import Mesh, PartitionSpec as P

TOKENS = 8192
DAMPING = 0.1
BLOCK = 512
TILE = 128
SIDE = BLOCK // TILE
UPPER = [(a, b) for a in range(SIDE) for b in range(a + 1, SIDE)]
PAIRS = range(0, SIDE, 2)
PACKED = (len(UPPER) + len(PAIRS)) * TILE
PEERS = 8
SHARE = PACKED // PEERS
PIECE = SHARE // PEERS
RAW = SIDE * TILE
DIAGONAL = 8
FIRST = RAW + SHARE + 2 * DIAGONAL
GATHER = SHARE + PIECE
SECOND = GATHER + PIECE + 4 * DIAGONAL
ROOT = PACKED + 2 * DIAGONAL
BF16, F32 = jnp.bfloat16, jnp.float32
AXES = ("x", "yl", "z", "yh", "c")
SIZES = (4, 2, 8, 4, 2)
VMEM = pl.BlockSpec(memory_space=pltpu.VMEM)
ANYWHERE = pl.BlockSpec(memory_space=pl.ANY)
PARAMS = pltpu.CompilerParams(vmem_limit_bytes=24 * 1024 * 1024)


def gram(data):
    return lax.dot_general(data, data, (((0,), (0,)), ((), ())), preferred_element_type=F32)


def tile_at(a, b):
    return slice(a * TILE, (a + 1) * TILE), slice(b * TILE, (b + 1) * TILE)


def over_diagonal():
    row = lax.broadcasted_iota(jnp.int32, (TILE, TILE), 0)
    return row < lax.broadcasted_iota(jnp.int32, (TILE, TILE), 1)


def pack(total, packed):
    tiles = [total[tile_at(a, b)] for a, b in UPPER]
    for a in PAIRS:
        first, second = total[tile_at(a, a)], total[tile_at(a + 1, a + 1)]
        tiles.append(jnp.where(over_diagonal(), first, second))
    for place, tile in enumerate(tiles):
        packed[place * TILE : (place + 1) * TILE, :] = tile.astype(packed.dtype)


def unpack(packed, full, ends):
    tiles = [packed[start : start + TILE, :].astype(F32) for start in range(0, PACKED, TILE)]
    for (a, b), tile in zip(UPPER, tiles):
        full[tile_at(a, b)] = tile.astype(full.dtype)
        full[tile_at(b, a)] = tile.T.astype(full.dtype)
    for a, tile in zip(PAIRS, tiles[len(UPPER) :]):
        turned = tile.T
        both = (tile, turned), (turned, tile)
        for place, (above, below) in enumerate(both, start=a):
            whole = jnp.where(over_diagonal(), above, below)
            whole = jnp.where(on_diagonal(TILE), ends[place : place + 1, :], whole)
            full[tile_at(place, place)] = whole.astype(full.dtype)


def halves(values):
    high = values.astype(BF16)
    return high, (values - high.astype(F32)).astype(BF16)


def product(left, right):
    left_high, left_low = left
    right_high, right_low = right
    dot = lambda p, q: jnp.dot(p, q, preferred_element_type=F32)
    return dot(left_high, right_high) + (dot(left_high, right_low) + dot(left_low, right_high))


def on_diagonal(count):
    row = lax.broadcasted_iota(jnp.int32, (count, count), 0)
    return row == lax.broadcasted_iota(jnp.int32, (count, count), 1)


def diagonals(total):
    parts = []
    for a in range(SIDE):
        tile = jnp.where(on_diagonal(TILE), total[tile_at(a, a)], 0.0)
        parts.append(jnp.sum(tile, axis=0, keepdims=True))
    return jnp.concatenate(parts + [jnp.zeros((DIAGONAL - SIDE, TILE), F32)], axis=0)


def inverse_root(covariance):
    diagonal = on_diagonal(BLOCK)
    shifted = covariance * (1.0 / TOKENS) + jnp.where(diagonal, DAMPING, 0.0)
    squares = jnp.sum(jnp.sum(shifted * shifted, axis=0, keepdims=True), axis=1, keepdims=True)
    frob = jnp.sqrt(squares)
    y = shifted * (1.0 / frob)
    y_halves = halves(y)
    s = product(y_halves, y_halves)
    tail = product(halves(s), halves(0.0625 * s - 0.5625 * y))
    z = jnp.where(diagonal, 2.25, 0.0) - 2.4375 * y + 1.6875 * s + tail
    return z * (1.0 / jnp.sqrt(frob))


def first_kernel(acts, grads, out, packed, ends):
    step = pl.program_id(0)

    @pl.when(step == 0)
    def _():
        total = gram(acts[...])
        pack(total, packed)
        high, low = halves(diagonals(total))
        ends[...] = jnp.concatenate([high, low], axis=0)

    count = out.shape[0]
    for place in range(count):
        for part in range(SIDE):
            column = place * BLOCK + part * TILE
            out[place, part * TILE : (part + 1) * TILE, :] = grads[:, column : column + TILE]
        start = pl.multiple_of((step * count + place) * SHARE, SHARE)
        out[place, RAW : RAW + SHARE, :] = packed[pl.ds(start, SHARE), :].astype(BF16)
        out[place, RAW + SHARE : FIRST, :] = ends[...]


def second_kernel(got, out, packed, share):
    tokens = jnp.concatenate(
        [got[:, p * TILE : (p + 1) * TILE, :].reshape(PEERS * TILE, TILE) for p in range(SIDE)],
        axis=1,
    )
    grad_total = gram(tokens)
    pack(grad_total, packed)
    total = jnp.zeros((SHARE, TILE), F32)
    ends = jnp.zeros((2 * DIAGONAL, TILE), F32)
    for peer in range(PEERS):
        total += got[peer, RAW : RAW + SHARE, :].astype(F32)
        ends += got[peer, RAW + SHARE : FIRST, :].astype(F32)
    share[...] = total
    grad_ends = halves(diagonals(grad_total))
    act_ends = halves(ends[0:DIAGONAL] + ends[DIAGONAL:])
    both = jnp.concatenate([*grad_ends, *act_ends], axis=0)
    for peer in range(PEERS):
        high, low = halves(share[peer * PIECE : (peer + 1) * PIECE, :])
        out[peer, 0:SHARE, :] = packed[peer * SHARE : (peer + 1) * SHARE, :].astype(BF16)
        out[peer, SHARE:GATHER, :] = high
        out[peer, GATHER : GATHER + PIECE, :] = low
        out[peer, GATHER + PIECE : SECOND, :] = both


def sum_kernel(got, out, ends):
    total = got[0].astype(F32)
    for peer in range(1, PEERS):
        total += got[peer].astype(F32)
    share = total[0:SHARE].astype(BF16)
    piece = (total[SHARE:GATHER] + total[GATHER : GATHER + PIECE]).astype(BF16)
    for peer in range(PEERS):
        out[peer, 0:SHARE, :] = share
        out[peer, SHARE:GATHER, :] = piece
    both = total[GATHER + PIECE : SECOND]
    ends[0:DIAGONAL, :] = both[0:DIAGONAL] + both[DIAGONAL : 2 * DIAGONAL]
    ends[DIAGONAL:, :] = both[2 * DIAGONAL : 3 * DIAGONAL] + both[3 * DIAGONAL :]


def grad_root_kernel(got, ends, out, full, packed):
    for peer in range(PEERS):
        packed[peer * SHARE : (peer + 1) * SHARE, :] = got[peer, 0:SHARE, :]
    unpack(packed, full, ends[0:DIAGONAL, :])
    root = inverse_root(full[...])
    pack(root, out)
    root_ends = diagonals(root)
    out[PACKED:, :] = jnp.concatenate([root_ends, root_ends], axis=0).astype(BF16)


def copies_kernel(got, out):
    for place in range(PEERS):
        piece = got[place, SHARE:GATHER, :]
        for peer in range(PEERS):
            out[peer, place * PIECE : (place + 1) * PIECE, :] = piece


def left_kernel(got, ends, grad, out, full):
    unpack(got, full, ends[DIAGONAL:, :])
    root = inverse_root(full[...]).astype(BF16)
    out[...] = jnp.dot(root, grad[...], preferred_element_type=F32).astype(BF16)


def last_kernel(left, root, out, full):
    unpack(root, full, root[PACKED:, :].astype(F32))
    out[...] = jnp.dot(left[...], full[...], preferred_element_type=F32)


def call(kernel, args, outs, scratch=(), flops=1 << 20, after=()):
    outs = [jax.ShapeDtypeStruct(dims, dtype) for dims, dtype in outs]
    data = sum(a.size * a.dtype.itemsize for a in [*args, *outs])

    def body(*refs):
        kernel(*refs[: len(args)], *refs[len(args) + len(after) :])

    got = pl.pallas_call(
        body,
        out_shape=outs,
        in_specs=[VMEM] * len(args) + [ANYWHERE] * len(after),
        out_specs=[VMEM] * len(outs),
        scratch_shapes=[pltpu.VMEM(dims, dtype) for dims, dtype in scratch],
        compiler_params=PARAMS,
        cost_estimate=pl.CostEstimate(flops=flops, bytes_accessed=data, transcendentals=0),
    )(*args, *after)
    return got if len(outs) > 1 else got[0]


def exchange(data, axes):
    return lax.all_to_all(data, axes, split_axis=0, concat_axis=0, tiled=True)


def transpose_places(data):
    places = np.arange(np.prod(SIZES)).reshape(SIZES)
    pairs = [
        (int(places[x, yl, z, yh, c]), int(places[yh, c, z, (x + yh) % 4, yl]))
        for x, yl, z, yh, c in np.ndindex(*SIZES)
    ]
    return lax.ppermute(data, AXES, pairs)


def on_device(acts, grads_out, grad):
    cube = 2 * BLOCK**3
    packed, full = (PACKED, TILE), (BLOCK, BLOCK)

    share = (SHARE, TILE)
    sent = pl.pallas_call(
        first_kernel,
        grid=(4,),
        out_shape=jax.ShapeDtypeStruct((PEERS, FIRST, TILE), BF16),
        in_specs=[
            pl.BlockSpec((TILE, BLOCK), lambda step: (0, 0)),
            pl.BlockSpec((TILE, 2 * BLOCK), lambda step: (0, step)),
        ],
        out_specs=pl.BlockSpec((2, FIRST, TILE), lambda step: (step, 0, 0)),
        scratch_shapes=[pltpu.VMEM(packed, F32), pltpu.VMEM((2 * DIAGONAL, TILE), BF16)],
        cost_estimate=pl.CostEstimate(flops=cube // 4, bytes_accessed=3 << 20, transcendentals=0),
    )(acts, grads_out)
    got = exchange(sent, "z")
    sent = call(
        second_kernel,
        [got],
        [((PEERS, SECOND, TILE), BF16)],
        [(packed, F32), (share, F32)],
        2 * cube,
    )
    got = exchange(sent, ("x", "yl"))
    sent, ends = call(
        sum_kernel, [got], [((PEERS, GATHER, TILE), BF16), ((2 * DIAGONAL, TILE), F32)]
    )
    got = exchange(sent, ("x", "yl"))
    root = call(
        grad_root_kernel,
        [got, ends],
        [((ROOT, TILE), BF16)],
        [(full, F32), (packed, BF16)],
        6 * cube,
    )
    grad_root = transpose_places(root)
    sent = call(copies_kernel, [got], [((PEERS, SHARE, TILE), BF16)], after=[root])
    act_cov = exchange(sent, "z").reshape(packed)
    left = call(left_kernel, [act_cov, ends, grad], [(full, BF16)], [(full, F32)], 7 * cube)
    return call(last_kernel, [left, grad_root], [(full, F32)], [(full, BF16)], cube)


def solution(mesh):
    split = Mesh(mesh.devices.reshape(SIZES), AXES)
    dp, tensor = AXES[:3], AXES[3:]
    return jax.shard_map(
        on_device,
        mesh=split,
        in_specs=(P(dp, tensor), P(dp, tensor), P(tensor, dp)),
        out_specs=P(tensor, dp),
        check_vma=False,
    )
```

```python
import jax
import jax.numpy as jnp
import numpy as np
from jax import lax
from jax.experimental import pallas as pl
from jax.experimental.pallas import tpu as pltpu
from jax.sharding import Mesh, PartitionSpec as P

TOKENS = 8192
DAMPING = 0.1
BLOCK = 512
TILE = 128
SIDE = BLOCK // TILE
UPPER = [(a, b) for a in range(SIDE) for b in range(a + 1, SIDE)]
PAIRS = range(0, SIDE, 2)
PACKED = (len(UPPER) + len(PAIRS)) * TILE
PEERS = 8
SHARE = PACKED // PEERS
PIECE = SHARE // PEERS
RAW = SIDE * TILE
DIAGONAL = 8
FIRST = RAW + SHARE + 2 * DIAGONAL
GATHER = SHARE + PIECE
SECOND = GATHER + PIECE + 4 * DIAGONAL
ROOT = PACKED + 2 * DIAGONAL
BF16, F32 = jnp.bfloat16, jnp.float32
AXES = ("x", "yl", "z", "yh", "c")
SIZES = (4, 2, 8, 4, 2)
VMEM = pl.BlockSpec(memory_space=pltpu.VMEM)
ANYWHERE = pl.BlockSpec(memory_space=pl.ANY)
PARAMS = pltpu.CompilerParams(vmem_limit_bytes=24 * 1024 * 1024)


def gram(data):
    return lax.dot_general(data, data, (((0,), (0,)), ((), ())), preferred_element_type=F32)


def tile_at(a, b):
    return slice(a * TILE, (a + 1) * TILE), slice(b * TILE, (b + 1) * TILE)


def over_diagonal():
    row = lax.broadcasted_iota(jnp.int32, (TILE, TILE), 0)
    return row < lax.broadcasted_iota(jnp.int32, (TILE, TILE), 1)


def pack(total, packed):
    tiles = [total[tile_at(a, b)] for a, b in UPPER]
    for a in PAIRS:
        first, second = total[tile_at(a, a)], total[tile_at(a + 1, a + 1)]
        tiles.append(jnp.where(over_diagonal(), first, second))
    for place, tile in enumerate(tiles):
        packed[place * TILE : (place + 1) * TILE, :] = tile.astype(packed.dtype)


def unpack(packed, full, ends):
    tiles = [packed[start : start + TILE, :].astype(F32) for start in range(0, PACKED, TILE)]
    for (a, b), tile in zip(UPPER, tiles):
        full[tile_at(a, b)] = tile.astype(full.dtype)
        full[tile_at(b, a)] = tile.T.astype(full.dtype)
    for a, tile in zip(PAIRS, tiles[len(UPPER) :]):
        turned = tile.T
        both = (tile, turned), (turned, tile)
        for place, (above, below) in enumerate(both, start=a):
            whole = jnp.where(over_diagonal(), above, below)
            whole = jnp.where(on_diagonal(TILE), ends[place : place + 1, :], whole)
            full[tile_at(place, place)] = whole.astype(full.dtype)


def halves(values):
    high = values.astype(BF16)
    return high, (values - high.astype(F32)).astype(BF16)


def product(left, right):
    left_high, left_low = left
    right_high, right_low = right
    dot = lambda p, q: jnp.dot(p, q, preferred_element_type=F32)
    return dot(left_high, right_high) + (dot(left_high, right_low) + dot(left_low, right_high))


def on_diagonal(count):
    row = lax.broadcasted_iota(jnp.int32, (count, count), 0)
    return row == lax.broadcasted_iota(jnp.int32, (count, count), 1)


def diagonals(total):
    parts = []
    for a in range(SIDE):
        tile = jnp.where(on_diagonal(TILE), total[tile_at(a, a)], 0.0)
        parts.append(jnp.sum(tile, axis=0, keepdims=True))
    return jnp.concatenate(parts + [jnp.zeros((DIAGONAL - SIDE, TILE), F32)], axis=0)


def inverse_root(covariance):
    diagonal = on_diagonal(BLOCK)
    shifted = covariance * (1.0 / TOKENS) + jnp.where(diagonal, DAMPING, 0.0)
    squares = jnp.sum(jnp.sum(shifted * shifted, axis=0, keepdims=True), axis=1, keepdims=True)
    frob = jnp.sqrt(squares)
    y = shifted * (1.0 / frob)
    y_halves = halves(y)
    s = product(y_halves, y_halves)
    tail = product(halves(s), halves(0.0625 * s - 0.5625 * y))
    z = jnp.where(diagonal, 2.25, 0.0) - 2.4375 * y + 1.6875 * s + tail
    return z * (1.0 / jnp.sqrt(frob))


def first_kernel(acts, grads, out, packed):
    total = gram(acts[...])
    pack(total, packed)
    high, low = halves(diagonals(total))
    ends = jnp.concatenate([high, low], axis=0)
    for peer in range(PEERS):
        for part in range(SIDE):
            column = peer * BLOCK + part * TILE
            out[peer, part * TILE : (part + 1) * TILE, :] = grads[:, column : column + TILE]
        share = packed[peer * SHARE : (peer + 1) * SHARE, :]
        out[peer, RAW : RAW + SHARE, :] = share.astype(BF16)
        out[peer, RAW + SHARE : FIRST, :] = ends


def second_kernel(got, out, packed, share):
    tokens = jnp.concatenate(
        [got[:, p * TILE : (p + 1) * TILE, :].reshape(PEERS * TILE, TILE) for p in range(SIDE)],
        axis=1,
    )
    grad_total = gram(tokens)
    pack(grad_total, packed)
    total = jnp.zeros((SHARE, TILE), F32)
    ends = jnp.zeros((2 * DIAGONAL, TILE), F32)
    for peer in range(PEERS):
        total += got[peer, RAW : RAW + SHARE, :].astype(F32)
        ends += got[peer, RAW + SHARE : FIRST, :].astype(F32)
    share[...] = total
    grad_ends = halves(diagonals(grad_total))
    act_ends = halves(ends[0:DIAGONAL] + ends[DIAGONAL:])
    both = jnp.concatenate([*grad_ends, *act_ends], axis=0)
    for peer in range(PEERS):
        high, low = halves(share[peer * PIECE : (peer + 1) * PIECE, :])
        out[peer, 0:SHARE, :] = packed[peer * SHARE : (peer + 1) * SHARE, :].astype(BF16)
        out[peer, SHARE:GATHER, :] = high
        out[peer, GATHER : GATHER + PIECE, :] = low
        out[peer, GATHER + PIECE : SECOND, :] = both


def sum_kernel(got, out, ends):
    total = got[0].astype(F32)
    for peer in range(1, PEERS):
        total += got[peer].astype(F32)
    share = total[0:SHARE].astype(BF16)
    piece = (total[SHARE:GATHER] + total[GATHER : GATHER + PIECE]).astype(BF16)
    for peer in range(PEERS):
        out[peer, 0:SHARE, :] = share
        out[peer, SHARE:GATHER, :] = piece
    both = total[GATHER + PIECE : SECOND]
    ends[0:DIAGONAL, :] = both[0:DIAGONAL] + both[DIAGONAL : 2 * DIAGONAL]
    ends[DIAGONAL:, :] = both[2 * DIAGONAL : 3 * DIAGONAL] + both[3 * DIAGONAL :]


def grad_root_kernel(got, ends, out, full, packed):
    for peer in range(PEERS):
        packed[peer * SHARE : (peer + 1) * SHARE, :] = got[peer, 0:SHARE, :]
    unpack(packed, full, ends[0:DIAGONAL, :])
    root = inverse_root(full[...])
    pack(root, out)
    root_ends = diagonals(root)
    out[PACKED:, :] = jnp.concatenate([root_ends, root_ends], axis=0).astype(BF16)


def copies_kernel(got, out):
    for place in range(PEERS):
        piece = got[place, SHARE:GATHER, :]
        for peer in range(PEERS):
            out[peer, place * PIECE : (place + 1) * PIECE, :] = piece


def left_kernel(got, ends, grad, out, full):
    unpack(got, full, ends[DIAGONAL:, :])
    root = inverse_root(full[...]).astype(BF16)
    out[...] = jnp.dot(root, grad[...], preferred_element_type=F32).astype(BF16)


def last_kernel(left, root, out, full):
    unpack(root, full, root[PACKED:, :].astype(F32))
    out[...] = jnp.dot(left[...], full[...], preferred_element_type=F32)


def call(kernel, args, outs, scratch=(), flops=1 << 20, after=()):
    outs = [jax.ShapeDtypeStruct(dims, dtype) for dims, dtype in outs]
    data = sum(a.size * a.dtype.itemsize for a in [*args, *outs])

    def body(*refs):
        kernel(*refs[: len(args)], *refs[len(args) + len(after) :])

    got = pl.pallas_call(
        body,
        out_shape=outs,
        in_specs=[VMEM] * len(args) + [ANYWHERE] * len(after),
        out_specs=[VMEM] * len(outs),
        scratch_shapes=[pltpu.VMEM(dims, dtype) for dims, dtype in scratch],
        compiler_params=PARAMS,
        cost_estimate=pl.CostEstimate(flops=flops, bytes_accessed=data, transcendentals=0),
    )(*args, *after)
    return got if len(outs) > 1 else got[0]


def exchange(data, axes):
    return lax.all_to_all(data, axes, split_axis=0, concat_axis=0, tiled=True)


MOVES = ((0, 2, 0, 2), (1, 1, 1, 1), (2, 0, 2, 0), (3, 3, 3, 3))


def transpose_places(data):
    places = np.arange(np.prod(SIZES)).reshape(SIZES)
    pairs = [
        (int(places[x, yl, z, yh, c]), int(places[yh, c, z, (yh + MOVES[x][yh]) % 4, yl]))
        for x, yl, z, yh, c in np.ndindex(*SIZES)
    ]
    return lax.ppermute(data, AXES, pairs)


def on_device(acts, grads_out, grad):
    cube = 2 * BLOCK**3
    packed, full = (PACKED, TILE), (BLOCK, BLOCK)

    share = (SHARE, TILE)
    sent = call(
        first_kernel,
        [acts, grads_out],
        [((PEERS, FIRST, TILE), BF16)],
        [(packed, F32)],
        cube // 4,
    )
    got = exchange(sent, "z")
    sent = call(
        second_kernel,
        [got],
        [((PEERS, SECOND, TILE), BF16)],
        [(packed, F32), (share, F32)],
        2 * cube,
    )
    got = exchange(sent, ("x", "yl"))
    sent, ends = call(
        sum_kernel, [got], [((PEERS, GATHER, TILE), BF16), ((2 * DIAGONAL, TILE), F32)]
    )
    got = exchange(sent, ("x", "yl"))
    root = call(
        grad_root_kernel,
        [got, ends],
        [((ROOT, TILE), BF16)],
        [(full, F32), (packed, BF16)],
        6 * cube,
    )
    grad_root = transpose_places(root)
    sent = call(copies_kernel, [got], [((PEERS, SHARE, TILE), BF16)], after=[root])
    act_cov = exchange(sent, "z").reshape(packed)
    left = call(left_kernel, [act_cov, ends, grad], [(full, BF16)], [(full, F32)], 7 * cube)
    return call(last_kernel, [left, grad_root], [(full, F32)], [(full, BF16)], cube)


def solution(mesh):
    split = Mesh(mesh.devices.reshape(SIZES), AXES)
    dp, tensor = AXES[:3], AXES[3:]
    return jax.shard_map(
        on_device,
        mesh=split,
        in_specs=(P(dp, tensor), P(dp, tensor), P(tensor, dp)),
        out_specs=P(tensor, dp),
        check_vma=False,
    )
```

```python
import jax
import jax.numpy as jnp
import numpy as np
from jax import lax
from jax.experimental import pallas as pl
from jax.experimental.pallas import tpu as pltpu
from jax.sharding import Mesh, PartitionSpec as P

TOKENS = 8192
DAMPING = 0.1
BLOCK = 512
TILE = 128
SIDE = BLOCK // TILE
UPPER = [(a, b) for a in range(SIDE) for b in range(a + 1, SIDE)]
PAIRS = range(0, SIDE, 2)
PACKED = (len(UPPER) + len(PAIRS)) * TILE
PEERS = 8
SHARE = PACKED // PEERS
PIECE = SHARE // PEERS
RAW = SIDE * TILE
DIAGONAL = 8
FIRST = RAW + SHARE + 2 * DIAGONAL
GATHER = SHARE + PIECE
SECOND = GATHER + PIECE + 4 * DIAGONAL
ROOT = PACKED + 2 * DIAGONAL
BF16, F32 = jnp.bfloat16, jnp.float32
AXES = ("x", "yl", "z", "yh", "c")
SIZES = (4, 2, 8, 4, 2)
VMEM = pl.BlockSpec(memory_space=pltpu.VMEM)
ANYWHERE = pl.BlockSpec(memory_space=pl.ANY)
PARAMS = pltpu.CompilerParams(vmem_limit_bytes=24 * 1024 * 1024)


def gram(data):
    return lax.dot_general(data, data, (((0,), (0,)), ((), ())), preferred_element_type=F32)


def tile_at(a, b):
    return slice(a * TILE, (a + 1) * TILE), slice(b * TILE, (b + 1) * TILE)


def over_diagonal():
    row = lax.broadcasted_iota(jnp.int32, (TILE, TILE), 0)
    return row < lax.broadcasted_iota(jnp.int32, (TILE, TILE), 1)


def pack(total, packed):
    tiles = [total[tile_at(a, b)] for a, b in UPPER]
    for a in PAIRS:
        first, second = total[tile_at(a, a)], total[tile_at(a + 1, a + 1)]
        tiles.append(jnp.where(over_diagonal(), first, second))
    for place, tile in enumerate(tiles):
        packed[place * TILE : (place + 1) * TILE, :] = tile.astype(packed.dtype)


def unpack(packed, full, ends):
    tiles = [packed[start : start + TILE, :].astype(F32) for start in range(0, PACKED, TILE)]
    for (a, b), tile in zip(UPPER, tiles):
        full[tile_at(a, b)] = tile.astype(full.dtype)
        full[tile_at(b, a)] = tile.T.astype(full.dtype)
    for a, tile in zip(PAIRS, tiles[len(UPPER) :]):
        turned = tile.T
        both = (tile, turned), (turned, tile)
        for place, (above, below) in enumerate(both, start=a):
            whole = jnp.where(over_diagonal(), above, below)
            whole = jnp.where(on_diagonal(TILE), ends[place : place + 1, :], whole)
            full[tile_at(place, place)] = whole.astype(full.dtype)


def halves(values):
    high = values.astype(BF16)
    return high, (values - high.astype(F32)).astype(BF16)


def product(left, right):
    left_high, left_low = left
    right_high, right_low = right
    dot = lambda p, q: jnp.dot(p, q, preferred_element_type=F32)
    return dot(left_high, right_high) + (dot(left_high, right_low) + dot(left_low, right_high))


def on_diagonal(count):
    row = lax.broadcasted_iota(jnp.int32, (count, count), 0)
    return row == lax.broadcasted_iota(jnp.int32, (count, count), 1)


def diagonals(total):
    parts = []
    for a in range(SIDE):
        tile = jnp.where(on_diagonal(TILE), total[tile_at(a, a)], 0.0)
        parts.append(jnp.sum(tile, axis=0, keepdims=True))
    return jnp.concatenate(parts + [jnp.zeros((DIAGONAL - SIDE, TILE), F32)], axis=0)


def inverse_root(covariance):
    diagonal = on_diagonal(BLOCK)
    shifted = covariance * (1.0 / TOKENS) + jnp.where(diagonal, DAMPING, 0.0)
    squares = jnp.sum(jnp.sum(shifted * shifted, axis=0, keepdims=True), axis=1, keepdims=True)
    frob = jnp.sqrt(squares)
    y = shifted * (1.0 / frob)
    y_halves = halves(y)
    s = product(y_halves, y_halves)
    tail = product(halves(s), halves(0.0625 * s - 0.5625 * y))
    z = jnp.where(diagonal, 2.25, 0.0) - 2.4375 * y + 1.6875 * s + tail
    return z * (1.0 / jnp.sqrt(frob))


def first_kernel(acts, grads, out, packed):
    total = gram(acts[...])
    pack(total, packed)
    high, low = halves(diagonals(total))
    ends = jnp.concatenate([high, low], axis=0)
    for peer in range(PEERS):
        for part in range(SIDE):
            column = peer * BLOCK + part * TILE
            out[peer, part * TILE : (part + 1) * TILE, :] = grads[:, column : column + TILE]
        share = packed[peer * SHARE : (peer + 1) * SHARE, :]
        out[peer, RAW : RAW + SHARE, :] = share.astype(BF16)
        out[peer, RAW + SHARE : FIRST, :] = ends


def second_kernel(got, out, packed, share):
    tokens = jnp.concatenate(
        [got[:, p * TILE : (p + 1) * TILE, :].reshape(PEERS * TILE, TILE) for p in range(SIDE)],
        axis=1,
    )
    grad_total = gram(tokens)
    pack(grad_total, packed)
    total = jnp.zeros((SHARE, TILE), F32)
    ends = jnp.zeros((2 * DIAGONAL, TILE), F32)
    for peer in range(PEERS):
        total += got[peer, RAW : RAW + SHARE, :].astype(F32)
        ends += got[peer, RAW + SHARE : FIRST, :].astype(F32)
    share[...] = total
    grad_ends = halves(diagonals(grad_total))
    act_ends = halves(ends[0:DIAGONAL] + ends[DIAGONAL:])
    both = jnp.concatenate([*grad_ends, *act_ends], axis=0)
    for peer in range(PEERS):
        high, low = halves(share[peer * PIECE : (peer + 1) * PIECE, :])
        out[peer, 0:SHARE, :] = packed[peer * SHARE : (peer + 1) * SHARE, :].astype(BF16)
        out[peer, SHARE:GATHER, :] = high
        out[peer, GATHER : GATHER + PIECE, :] = low
        out[peer, GATHER + PIECE : SECOND, :] = both


def sum_kernel(got, out, ends):
    total = got[0].astype(F32)
    for peer in range(1, PEERS):
        total += got[peer].astype(F32)
    share = total[0:SHARE].astype(BF16)
    piece = (total[SHARE:GATHER] + total[GATHER : GATHER + PIECE]).astype(BF16)
    for peer in range(PEERS):
        out[peer, 0:SHARE, :] = share
        out[peer, SHARE:GATHER, :] = piece
    both = total[GATHER + PIECE : SECOND]
    ends[0:DIAGONAL, :] = both[0:DIAGONAL] + both[DIAGONAL : 2 * DIAGONAL]
    ends[DIAGONAL:, :] = both[2 * DIAGONAL : 3 * DIAGONAL] + both[3 * DIAGONAL :]


def grad_root_kernel(got, ends, out, full, packed):
    for peer in range(PEERS):
        packed[peer * SHARE : (peer + 1) * SHARE, :] = got[peer, 0:SHARE, :]
    unpack(packed, full, ends[0:DIAGONAL, :])
    root = inverse_root(full[...])
    pack(root, out)
    root_ends = diagonals(root)
    out[PACKED:, :] = jnp.concatenate([root_ends, root_ends], axis=0).astype(BF16)


def copies_kernel(got, out):
    for place in range(PEERS):
        piece = got[place, SHARE:GATHER, :]
        for peer in range(PEERS):
            out[peer, place * PIECE : (place + 1) * PIECE, :] = piece


def left_kernel(got, ends, grad, out, full):
    unpack(got, full, ends[DIAGONAL:, :])
    root = inverse_root(full[...]).astype(BF16)
    out[...] = jnp.dot(root, grad[...], preferred_element_type=F32).astype(BF16)


def last_kernel(left, root, out, full):
    unpack(root, full, root[PACKED:, :].astype(F32))
    out[...] = jnp.dot(left[...], full[...], preferred_element_type=F32)


def call(kernel, args, outs, scratch=(), flops=1 << 20, after=()):
    outs = [jax.ShapeDtypeStruct(dims, dtype) for dims, dtype in outs]
    data = sum(a.size * a.dtype.itemsize for a in [*args, *outs])

    def body(*refs):
        kernel(*refs[: len(args)], *refs[len(args) + len(after) :])

    got = pl.pallas_call(
        body,
        out_shape=outs,
        in_specs=[VMEM] * len(args) + [ANYWHERE] * len(after),
        out_specs=[VMEM] * len(outs),
        scratch_shapes=[pltpu.VMEM(dims, dtype) for dims, dtype in scratch],
        compiler_params=PARAMS,
        cost_estimate=pl.CostEstimate(flops=flops, bytes_accessed=data, transcendentals=0),
    )(*args, *after)
    return got if len(outs) > 1 else got[0]


def exchange(data, axes):
    return lax.all_to_all(data, axes, split_axis=0, concat_axis=0, tiled=True)


MOVES = ((0, 2, 0, 2), (1, 1, 1, 1), (2, 0, 2, 0), (3, 3, 3, 3))


def transpose_places(data):
    places = np.arange(np.prod(SIZES)).reshape(SIZES)
    pairs = [
        (int(places[x, yl, z, yh, c]), int(places[yh, c, z, (yh + MOVES[x][yh]) % 4, yl]))
        for x, yl, z, yh, c in np.ndindex(*SIZES)
    ]
    return lax.ppermute(data, AXES, pairs)


def on_device(acts, grads_out, grad):
    cube = 2 * BLOCK**3
    packed, full = (PACKED, TILE), (BLOCK, BLOCK)

    share = (SHARE, TILE)
    sent = call(
        first_kernel,
        [acts, grads_out],
        [((PEERS, FIRST, TILE), BF16)],
        [(packed, F32)],
        cube // 4,
    )
    got = exchange(sent, "z")
    sent = call(
        second_kernel,
        [got],
        [((PEERS, SECOND, TILE), BF16)],
        [(packed, F32), (share, F32)],
        2 * cube,
    )
    got = exchange(sent, ("x", "yl"))
    sent, ends = call(
        sum_kernel, [got], [((PEERS, GATHER, TILE), BF16), ((2 * DIAGONAL, TILE), F32)]
    )
    got = exchange(sent, ("x", "yl"))
    sent = call(copies_kernel, [got], [((PEERS, SHARE, TILE), BF16)])
    root = call(
        grad_root_kernel,
        [got, ends],
        [((ROOT, TILE), BF16)],
        [(full, F32), (packed, BF16)],
        6 * cube,
        [sent],
    )
    grad_root = transpose_places(root)
    act_cov = exchange(sent, "z").reshape(packed)
    left = call(left_kernel, [act_cov, ends, grad], [(full, BF16)], [(full, F32)], 7 * cube)
    return call(last_kernel, [left, grad_root], [(full, F32)], [(full, BF16)], cube)


def solution(mesh):
    split = Mesh(mesh.devices.reshape(SIZES), AXES)
    dp, tensor = AXES[:3], AXES[3:]
    return jax.shard_map(
        on_device,
        mesh=split,
        in_specs=(P(dp, tensor), P(dp, tensor), P(tensor, dp)),
        out_specs=P(tensor, dp),
        check_vma=False,
    )
```
